32 devices in a mesh: groups: 2 (over y), ctx: 4 (over z), roll: 4 (over x, core).
Axes of the slice: x: 2, y: 2, z: 4, core: 2. Of those that a mesh axis runs over, the one named last changes fastest.
Arguments:
- queries: bfloat16 [4096, 8192], P(('groups', 'ctx', 'roll')), parts along dimension 0, may hold values from -1.6953125 to 1.6953125
- cotangent: bfloat16 [4096, 8192], P(('groups', 'ctx', 'roll')), parts along dimension 0, may hold values from -6 to 6
- out_dot: float32 [4096, 64], P(('groups', 'ctx', 'roll')), parts along dimension 0, may hold values from -48 to 48
- norm_offset: float32 [4096, 64], P(('groups', 'ctx', 'roll')), parts along dimension 0, may hold values from 0.5 to 2.5
- prompt_kv: bfloat16 [2, 512, 1024], P(None, ('groups', 'ctx')), parts along dimension 1, may hold values from -1.6953125 to 1.6953125
- prompt_x: bfloat16 [512, 8192], P(('groups', 'ctx')), parts along dimension 0, may hold values from -6 to 6
- block_ids: int32 [128], P(('groups', 'ctx', 'roll')), parts along dimension 0, may hold values from 0 to 63, each once
- lengths: int32 [32], P('groups'), parts along dimension 0, may hold values from 32 to 128, as said below
- advantages: float32 [32], P('groups'), parts along dimension 0, may hold values from -3 to 3
- adv_index: int32 [32], P('groups'), parts along dimension 0, may hold values from 0 to 15, each once
Outputs:
- query_grad: bfloat16 [4096, 8192], P(('groups', 'ctx', 'roll')), parts along dimension 0
- kv_grad: float32 [2, 512, 1024], P(None, ('groups', 'ctx'), 'roll'), parts along dimension 1
- kv_weight_grad: float32 [2, 16384, 1024], P(None, ('groups', 'ctx'), 'roll'), parts along dimension 1
The draws below stay inside these ranges and needn't reach their ends.
There are 2 independent parts, one for each index of `groups`. The reference program is written for one: setup_inputs(seed, part) draws one part's arguments, and reference() takes and returns one part's arrays. A program takes and returns all parts, laid end to end along the dimension named above; each array names one. Nothing has to cross between parts.
Inputs may be any that keep to these rules, and one draw needn't show every extreme that they name: `lengths`: every rollout has a length of at least 32, and some rollout has length 128. `block_ids`: each id appears once. `adv_index`: each entry appears once.
All inputs are finite; a program needn't handle non-finite values.
Results may differ from the reference program's by a relative error of at most 0.0057.
Values may be sent and summed in bfloat16 or wider, within the bound.
No kernel may reach another device: no remote copies, remote signals or barrier semaphores. Data moves between devices by JAX's collectives and lax.ppermute only.
A program may use at most 128 MiB of HBM per device.

```python
import math
import jax
import jax.numpy as jnp
from jax import lax

D = 8192
H = 64
KVH = 8
HD = 128
BLOCK = 32
ROLLOUTS = 16
SLAB = 256
RTOK = 2048
RESP_MAX = 128
BPR = 4
NBLK = 64


def draw_lengths(key, part):
    first, second = jax.random.split(jax.random.fold_in(key, 11))
    values = jax.random.randint(first, (ROLLOUTS,), RESP_MAX // 4, RESP_MAX + 1, dtype=jnp.int32)
    chosen = jax.random.randint(second, (), 0, ROLLOUTS, dtype=jnp.int32)
    places = jnp.arange(ROLLOUTS, dtype=jnp.int32)
    return jnp.where(places == chosen, jnp.int32(RESP_MAX), values).astype(jnp.int32)


def block_scale(key, shape, pieces, low, high):
    def one(dim, parts):
        draws = jax.random.uniform(jax.random.fold_in(jax.random.fold_in(key, 6), dim), (parts,), jnp.float32, low / len(pieces), high / len(pieces))
        return jnp.repeat(jnp.exp(draws), shape[dim] // parts).reshape((-1,) + (1,) * (len(shape) - dim - 1))

    loudness = one(*pieces[0])
    for cut in pieces[1:]:
        loudness = loudness * one(*cut)
    return loudness


def scatter_about(own_key, shape, scale, limit, cuts=(), held_as=jnp.bfloat16):
    values = jax.random.normal(own_key, shape, jnp.float32) * scale
    if len(cuts) > 0:
        values = block_scale(own_key, shape, cuts, -0.22, 0.18) * values
    return jnp.clip(values, min=-limit, max=limit).astype(held_as)


def setup_inputs(seed: int = 0, part: int = 0) -> dict:
    streams_of = jax.random.split(jax.random.key(seed), 11)
    part_splits = jax.random.split(jax.random.fold_in(streams_of[10], part), 11)
    queries = jnp.clip(jax.random.uniform(part_splits[0], (RTOK, H * HD), jnp.float32, -1.6953125, 1.6953125) * block_scale(part_splits[0], (RTOK, H * HD), ((0, 16),), -0.4, 0.0), -1.6953125, 1.6953125).astype(jnp.bfloat16)
    cotangent = scatter_about(part_splits[1], (RTOK, H * HD), 1.0, 6.0, ((0, 16),))
    out_dot = scatter_about(part_splits[2], (RTOK, H), 8.0, 48.0, ((0, 16),), jnp.float32)
    norm_offset = jnp.clip(0.5 + 2.0 * jax.random.uniform(part_splits[3], (RTOK, H), jnp.float32) ** block_scale(part_splits[3], (RTOK, H), ((0, 16),), -0.2, 0.2), 0.5, 2.5)
    prompt_kv = jnp.clip(jax.random.uniform(part_splits[4], (2, SLAB, KVH * HD), jnp.float32, -1.6953125, 1.6953125) * block_scale(part_splits[4], (2, SLAB, KVH * HD), ((1, 4),), -0.4, 0.0), -1.6953125, 1.6953125).astype(jnp.bfloat16)
    prompt_x = scatter_about(part_splits[5], (SLAB, D), 1.0, 6.0, ((0, 4),))
    block_ids = jax.random.permutation(part_splits[6], NBLK).astype(jnp.int32)
    lengths = draw_lengths(jax.random.fold_in(jax.random.fold_in(streams_of[10], part), 71), part)
    advantages = scatter_about(part_splits[8], (ROLLOUTS,), 1.0, 3.0, (), jnp.float32)
    adv_index = jax.random.permutation(part_splits[9], ROLLOUTS).astype(jnp.int32)
    return dict(queries=queries, cotangent=cotangent, out_dot=out_dot, norm_offset=norm_offset, prompt_kv=prompt_kv, prompt_x=prompt_x, block_ids=block_ids, lengths=lengths, advantages=advantages, adv_index=adv_index)


def rollout_weights(block_ids, lengths, advantages, adv_index):
    count = lengths.shape[0]
    rollout = block_ids // BPR
    slot = block_ids % BPR
    picks = rollout[:, None] == jnp.arange(count, dtype=jnp.int32)[None, :]
    length_of = lax.optimization_barrier(jnp.sum(jnp.where(picks, lengths[None, :], 0), axis=1))
    table = adv_index[:, None] == jnp.arange(count, dtype=jnp.int32)[None, :]
    adv_rollout = lax.optimization_barrier(jnp.sum(jnp.where(table, advantages[None, :], jnp.float32(0.0)), axis=1))
    adv_block = lax.optimization_barrier(jnp.sum(jnp.where(picks, adv_rollout[None, :], jnp.float32(0.0)), axis=1))
    position = slot[:, None] * BLOCK + jnp.arange(BLOCK, dtype=jnp.int32)[None, :]
    scaled = adv_block * RESP_MAX / length_of.astype(jnp.float32)
    weights = jnp.where(position < length_of[:, None], scaled[:, None], jnp.float32(0.0))
    return weights.reshape(-1)

def spread(x, groups):
    tokens = x.shape[0]
    return x.reshape(tokens, KVH, groups, -1).transpose(1, 0, 2, 3).reshape(KVH, tokens * groups, -1)

def reference(queries, cotangent, out_dot, norm_offset, prompt_kv, prompt_x, block_ids, lengths, advantages, adv_index):
    tokens = queries.shape[0]
    groups = H // KVH
    scale = 1.0 / math.sqrt(HD)
    weights = rollout_weights(block_ids, lengths, advantages, adv_index)
    grad_out = (cotangent.astype(jnp.float32) * weights[:, None]).astype(jnp.bfloat16)
    grad_out = lax.optimization_barrier(grad_out)
    delta = weights[:, None] * out_dot
    q_heads = spread(queries.astype(jnp.float32), groups)
    do_heads = spread(grad_out.astype(jnp.float32), groups)
    d_heads = spread(delta[:, :, None], groups)[:, :, 0]
    o_heads = spread(norm_offset[:, :, None], groups)[:, :, 0]
    kv_heads = prompt_kv.astype(jnp.float32).reshape(2, SLAB, KVH, HD).transpose(0, 2, 1, 3)
    rows = tokens * groups
    block = math.gcd(rows, 4096)
    count = rows // block

    def per_head(args):
        qg, dog, dg, og, kg, vg = args

        def per_block(carry, blk):
            qb, dob, db, ob = blk
            scores = jnp.dot(qb, kg.T, precision=lax.Precision.HIGHEST) * scale
            prob = jnp.exp(scores - ob[:, None]) / SLAB
            prob_low = lax.optimization_barrier(prob.astype(jnp.bfloat16)).astype(jnp.float32)
            dprob = jnp.dot(dob, vg.T, precision=lax.Precision.HIGHEST)
            dscore = (prob * (dprob - db[:, None]) * scale).astype(jnp.bfloat16)
            dscore = lax.optimization_barrier(dscore).astype(jnp.float32)
            dq = jnp.dot(dscore, kg, precision=lax.Precision.HIGHEST)
            dk = carry[0] + jnp.dot(dscore.T, qb, precision=lax.Precision.HIGHEST)
            dv = carry[1] + jnp.dot(prob_low.T, dob, precision=lax.Precision.HIGHEST)
            return ((dk, dv), dq)
        init = (jnp.zeros((SLAB, HD), jnp.float32), jnp.zeros((SLAB, HD), jnp.float32))
        blocks = (qg.reshape(count, block, HD), dog.reshape(count, block, HD), dg.reshape(count, block), og.reshape(count, block))
        (dk, dv), dq = lax.scan(per_block, init, blocks)
        return (dq.reshape(rows, HD), dk, dv)
    dq, dk, dv = lax.map(per_head, (q_heads, do_heads, d_heads, o_heads, kv_heads[0], kv_heads[1]))
    query_grad = dq.reshape(KVH, tokens, groups, HD).transpose(1, 0, 2, 3).reshape(tokens, H * HD).astype(jnp.bfloat16)
    kv_grad = jnp.stack([dk, dv]).transpose(0, 2, 1, 3).reshape(2, SLAB, KVH * HD)
    kv_low = lax.optimization_barrier(kv_grad.astype(jnp.bfloat16)).astype(jnp.float32)
    x_wide = prompt_x.astype(jnp.float32)
    key_w = jnp.dot(x_wide.T, kv_low[0], precision=lax.Precision.HIGHEST)
    value_w = jnp.dot(x_wide.T, kv_low[1], precision=lax.Precision.HIGHEST)
    return (query_grad, kv_grad, jnp.stack([key_w, value_w]))
```

```python
import functools
import math

import jax
import jax.numpy as jnp
from jax import lax
from jax.experimental import pallas as pl
from jax.experimental.pallas import tpu as pltpu
from jax.sharding import PartitionSpec as P

HD = 128
BLOCK = 32
MIB = 2**20
NT = (((1,), (1,)), ((), ()))
TN = (((0,), (0,)), ((), ()))
F32 = jnp.float32
BF16 = jnp.bfloat16


def xor_pairs(count, offset):
    return [(i, i ^ offset) for i in range(count)]


def prep_kernel(per_rollout, slab, ids, lengths, advantages, adv_index, ct_ref, od_ref, no_ref, go_ref, d_ref, o_ref):
    resp_max = per_rollout * BLOCK
    rows = []
    for b in range(ids.shape[0]):
        rollout = ids[b] // per_rollout
        slot = ids[b] % per_rollout
        length = lengths[rollout]
        scaled = jnp.full((BLOCK, HD), advantages[adv_index[rollout]] * resp_max, F32) / jnp.full(
            (BLOCK, HD), length.astype(F32), F32
        )
        position = slot * BLOCK + lax.broadcasted_iota(jnp.int32, (BLOCK, HD), 0)
        rows.append(jnp.where(position < length, scaled, jnp.float32(0.0)))
    weights = jnp.concatenate(rows, 0)
    heads = od_ref.shape[1]

    @pl.when(pl.program_id(0) == 0)
    def _():
        d_ref[...] = jnp.transpose(weights[:, :heads] * od_ref[...])
        o_ref[...] = jnp.transpose(no_ref[...] * math.log2(math.e) + math.log2(slab))

    for c in range(ct_ref.shape[1] // HD):
        cols = slice(c * HD, (c + 1) * HD)
        go_ref[:, cols] = (ct_ref[:, cols].astype(F32) * weights).astype(BF16)


def prep(per_rollout, slab, ids, lengths, advantages, adv_index, cotangent, out_dot, norm_offset):
    tokens, width = cotangent.shape
    heads = out_dot.shape[1]
    step = 2048
    small = pl.BlockSpec((tokens, heads), lambda i, *_: (0, 0))
    turned = pl.BlockSpec((heads, tokens), lambda i, *_: (0, 0))
    wide = pl.BlockSpec((tokens, step), lambda i, *_: (0, i))
    return pl.pallas_call(
        functools.partial(prep_kernel, per_rollout, slab),
        grid_spec=pltpu.PrefetchScalarGridSpec(
            num_scalar_prefetch=4,
            grid=(width // step,),
            in_specs=[wide, small, small],
            out_specs=[wide, turned, turned],
        ),
        out_shape=[
            jax.ShapeDtypeStruct((tokens, width), BF16),
            jax.ShapeDtypeStruct((heads, tokens), F32),
            jax.ShapeDtypeStruct((heads, tokens), F32),
        ],
        compiler_params=pltpu.CompilerParams(vmem_limit_bytes=8 * MIB),
        name="prep",
    )(ids, lengths, advantages, adv_index, cotangent, out_dot, norm_offset)


def heads_kernel(pieces, per_kv, aliased, block_ref, q_ref, go_ref, o_ref, d_ref, *refs):
    kv_refs = refs[:pieces]
    dq_ref, grads_ref = refs[pieces + aliased :]
    tokens = q_ref.shape[0]
    rows = kv_refs[0].shape[1]
    scale = 1.0 / math.sqrt(HD)
    keys = jnp.concatenate([r[0] for r in kv_refs], 0)
    values = jnp.concatenate([r[1] for r in kv_refs], 0)
    cols = [slice(h * HD, (h + 1) * HD) for h in range(per_kv)]
    q = jnp.concatenate([q_ref[:, c] for c in cols], 0)
    go = jnp.concatenate([go_ref[:, c] for c in cols], 0)
    offset = jnp.concatenate([o_ref[h : h + 1, :] for h in range(per_kv)], 1)
    delta = jnp.concatenate([d_ref[h : h + 1, :] for h in range(per_kv)], 1)
    scores = lax.dot_general(keys, q, NT, preferred_element_type=F32)
    prob = jnp.exp2(scores * (scale * math.log2(math.e)) - offset)
    dprob = lax.dot_general(values, go, NT, preferred_element_type=F32)
    dscore = ((prob * scale) * (dprob - delta)).astype(BF16)
    dq = lax.dot_general(dscore, keys, TN, preferred_element_type=F32).astype(BF16)
    for h in range(per_kv):
        dq_ref[:, cols[h]] = dq[h * tokens : (h + 1) * tokens]
    dk = jnp.dot(dscore, q, preferred_element_type=F32)
    dv = jnp.dot(prob.astype(BF16), go, preferred_element_type=F32)
    for c in range(pieces):
        span = slice(c * rows, (c + 1) * rows)
        grads_ref[c, 0] = dk[span].astype(grads_ref.dtype)
        grads_ref[c, 1] = dv[span].astype(grads_ref.dtype)


def head_block(block, kv_width, queries, grad_out, offset, delta, kv, dq, out_type):
    tokens, width = queries.shape
    _, rows, cols = kv[0].shape
    pieces = len(kv)
    count = cols // HD
    per_kv = queries.shape[1] // kv_width
    wide = pl.BlockSpec((tokens, per_kv * HD), lambda g, b: (0, b[0] * count + g))
    small = pl.BlockSpec((per_kv, tokens), lambda g, b: (b[0] * count + g, 0))
    piece = pl.BlockSpec((2, rows, HD), lambda g, b: (0, 0, g))
    aliased = int(dq is not None)
    slab = rows * pieces
    products = 5 * tokens * per_kv * slab * HD * count
    return pl.pallas_call(
        functools.partial(heads_kernel, pieces, per_kv, aliased),
        grid_spec=pltpu.PrefetchScalarGridSpec(
            num_scalar_prefetch=1,
            grid=(count,),
            in_specs=[wide, wide, small, small]
            + [piece] * pieces
            + [pl.BlockSpec(memory_space=pl.ANY)] * aliased,
            out_specs=[wide, pl.BlockSpec((pieces, 2, rows, HD), lambda g, b: (0, 0, 0, g))],
        ),
        out_shape=[
            jax.ShapeDtypeStruct((tokens, width), BF16),
            jax.ShapeDtypeStruct((pieces, 2, rows, cols), out_type),
        ],
        input_output_aliases={5 + pieces: 0} if aliased else {},
        compiler_params=pltpu.CompilerParams(vmem_limit_bytes=12 * MIB + slab * 32 * 1024),
        cost_estimate=pl.CostEstimate(
            flops=2 * products,
            bytes_accessed=tokens * per_kv * HD * count * 6,
            transcendentals=tokens * per_kv * slab * count,
        ),
        name="head_block",
    )(block, queries, grad_out, offset, delta, *kv, *([dq] if aliased else []))


def turn_kernel(pieces, *refs):
    x = jnp.concatenate([r[...] for r in refs[:pieces]], 0)
    refs[pieces][...] = jnp.transpose(x)


def turn(x):
    rows, cols = x[0].shape
    step = min(cols, 512)
    return pl.pallas_call(
        functools.partial(turn_kernel, len(x)),
        grid=(cols // step,),
        in_specs=[pl.BlockSpec((rows, step), lambda i: (0, i))] * len(x),
        out_specs=pl.BlockSpec((step, rows * len(x)), lambda i: (i, 0)),
        out_shape=jax.ShapeDtypeStruct((cols, rows * len(x)), BF16),
        compiler_params=pltpu.CompilerParams(vmem_limit_bytes=12 * MIB),
        name="turn_hidden",
    )(*x)


def weight_kernel(pieces, steps, core_ref, mine_ref, other_ref, *refs):
    low = refs[:pieces]
    out_ref = refs[pieces]
    keys = jnp.concatenate([r[0] for r in low], 0)
    values = jnp.concatenate([r[1] for r in low], 0)

    def write(x):
        out_ref[0] = jnp.dot(x, keys, preferred_element_type=F32)
        out_ref[1] = jnp.dot(x, values, preferred_element_type=F32)

    @pl.when(pl.program_id(0) < steps)
    def _():
        write(mine_ref[...])

    @pl.when(pl.program_id(0) >= steps)
    def _():
        write(other_ref[...])


def weight_grads(core, mine, other, low):
    half, slab = mine.shape
    _, rows, cols = low[0].shape
    step = min(half, 512)
    steps = half // step

    def place(i, core):
        return (0, (i // steps ^ core[0]) * steps + i % steps, 0)

    return pl.pallas_call(
        functools.partial(weight_kernel, len(low), steps),
        grid_spec=pltpu.PrefetchScalarGridSpec(
            num_scalar_prefetch=1,
            grid=(2 * steps,),
            in_specs=[
                pl.BlockSpec((step, slab), lambda i, core: (jnp.minimum(i, steps - 1), 0)),
                pl.BlockSpec((step, slab), lambda i, core: (jnp.maximum(i - steps, 0), 0)),
            ]
            + [pl.BlockSpec((2, rows, cols), lambda i, core: (0, 0, 0))] * len(low),
            out_specs=pl.BlockSpec((2, step, cols), place),
        ),
        out_shape=jax.ShapeDtypeStruct((2, 2 * half, cols), F32),
        compiler_params=pltpu.CompilerParams(vmem_limit_bytes=16 * MIB),
        name="weight_grads",
    )(core, mine, other, *low)


def on_device(
    queries,
    cotangent,
    out_dot,
    norm_offset,
    prompt_kv,
    prompt_x,
    block_ids,
    lengths,
    advantages,
    adv_index,
):
    ctx_count = lax.axis_size("ctx")
    roll_count = lax.axis_size("roll")
    ctx = lax.axis_index("ctx")
    roll = lax.axis_index("roll")
    core = roll % 2
    _, rows, kv_width = prompt_kv.shape
    cols = kv_width // roll_count
    slab = rows * ctx_count

    def to_ctx(x, offset):
        return lax.ppermute(x, "ctx", xor_pairs(ctx_count, offset))

    def to_roll(x, offset):
        return lax.ppermute(x, "roll", xor_pairs(roll_count, offset))

    last = roll_count - 1
    own = lax.dynamic_slice_in_dim(prompt_kv, (roll ^ last) * cols, cols, 2)
    fetched = [own] + [to_ctx(own, k) for k in range(1, ctx_count)]
    kv = {last: fetched}
    stacked = jnp.stack(fetched)
    blocks = {last: stacked}
    blocks[last - 1] = to_roll(stacked, 1)
    for d in range(1, roll_count // 2):
        blocks[last - 2 * d] = to_roll(stacked, 2 * d)
        blocks[last - 2 * d - 1] = to_roll(blocks[last - 2 * d], 1)
    for off in blocks:
        if off != last:
            kv[off] = [blocks[off][c] for c in range(ctx_count)]

    blocks_total = block_ids.shape[0] * ctx_count * roll_count
    grad_out, delta, offset = prep(
        blocks_total // lengths.shape[0], slab, block_ids, lengths, advantages, adv_index, cotangent, out_dot, norm_offset
    )

    width = prompt_x.shape[1] // ctx_count
    half = width // 2
    part = [
        lax.dynamic_slice_in_dim(prompt_x, (ctx ^ k) * width + core * half, half, 1)
        for k in range(ctx_count)
    ]
    x_mine = turn([part[0]] + [to_ctx(part[k], k) for k in range(1, ctx_count)])
    x_other = to_roll(x_mine, 1)

    dq = None
    arrived = []
    for d in reversed(range(roll_count // 2)):
        sums = {}
        for off, kind in ((2 * d + 1, BF16), (2 * d, F32)):
            dq, sums[off] = head_block(
                (roll ^ off)[None].astype(jnp.int32), kv_width, queries, grad_out, offset, delta, kv[off], dq, kind
            )
        total = sums[2 * d] + to_roll(sums[2 * d + 1], 1).astype(F32)
        if d:
            arrived.append(to_roll(total.astype(BF16), 2 * d))
    for part_sum in arrived:
        total = total + part_sum.astype(F32)
    owned = total[0]
    low_total = total.astype(BF16)
    for k in range(1, ctx_count):
        owned = owned + to_ctx(low_total[k], k).astype(F32)
    owned_low = owned.astype(BF16)
    low = [owned_low] + [to_ctx(owned_low, k) for k in range(1, ctx_count)]
    weight_grad = weight_grads(core[None].astype(jnp.int32), x_mine, x_other, low)
    return (dq, owned, weight_grad)


def solution(mesh):
    placed = (
        P(("groups", "ctx", "roll"), None),
        P(("groups", "ctx", "roll"), None),
        P(("groups", "ctx", "roll"), None),
        P(("groups", "ctx", "roll"), None),
        P(None, ("groups", "ctx"), None),
        P(("groups", "ctx"), None),
        P(("groups", "ctx", "roll")),
        P("groups"),
        P("groups"),
        P("groups"),
    )
    return jax.shard_map(
        on_device,
        mesh=mesh,
        in_specs=placed,
        out_specs=(
            P(("groups", "ctx", "roll"), None),
            P(None, ("groups", "ctx"), "roll"),
            P(None, ("groups", "ctx"), "roll"),
        ),
        check_vma=False,
    )
```

```python
import functools
import math

import jax
import jax.numpy as jnp
from jax import lax
from jax.experimental import pallas as pl
from jax.experimental.pallas import tpu as pltpu
from jax.sharding import PartitionSpec as P

HD = 128
BLOCK = 32
MIB = 2**20
NT = (((1,), (1,)), ((), ()))
TN = (((0,), (0,)), ((), ()))
F32 = jnp.float32
BF16 = jnp.bfloat16
WHOLE = pl.BlockSpec(memory_space=pltpu.VMEM)


def xor_pairs(count, offset):
    return [(i, i ^ offset) for i in range(count)]


def prep_kernel(per_rollout, slab, ids, lengths, advantages, adv_index, od_ref, no_ref, w_ref, d_ref, o_ref):
    resp_max = per_rollout * BLOCK
    rows = []
    for b in range(ids.shape[0]):
        rollout = ids[b] // per_rollout
        slot = ids[b] % per_rollout
        length = lengths[rollout]
        scaled = jnp.full((BLOCK, HD), advantages[adv_index[rollout]] * resp_max, F32) / jnp.full(
            (BLOCK, HD), length.astype(F32), F32
        )
        position = slot * BLOCK + lax.broadcasted_iota(jnp.int32, (BLOCK, HD), 0)
        rows.append(jnp.where(position < length, scaled, jnp.float32(0.0)))
    weights = jnp.concatenate(rows, 0)
    w_ref[...] = weights
    d_ref[...] = jnp.transpose(weights)[: od_ref.shape[0]] * od_ref[...]
    o_ref[...] = no_ref[...] * math.log2(math.e) + math.log2(slab)


def prep(per_rollout, slab, ids, lengths, advantages, adv_index, out_dot, norm_offset):
    heads, tokens = out_dot.shape
    scalars = pl.BlockSpec(memory_space=pltpu.SMEM)
    return pl.pallas_call(
        functools.partial(prep_kernel, per_rollout, slab),
        in_specs=[scalars] * 4 + [WHOLE] * 2,
        out_specs=[WHOLE] * 3,
        out_shape=[
            jax.ShapeDtypeStruct((tokens, HD), F32),
            jax.ShapeDtypeStruct((heads, tokens), F32),
            jax.ShapeDtypeStruct((heads, tokens), F32),
        ],
        compiler_params=pltpu.CompilerParams(vmem_limit_bytes=4 * MIB),
        cost_estimate=pl.CostEstimate(flops=2**30, bytes_accessed=0, transcendentals=0),
        name="prep",
    )(ids, lengths, advantages, adv_index, out_dot, norm_offset)


def heads_kernel(per_kv, off, q_ref, ct_ref, w_ref, o_ref, d_ref, kv_ref, dq_ref, grads_ref):
    tokens = q_ref.shape[0]
    pieces, _, rows, cols = kv_ref.shape
    count = cols // HD
    span = per_kv * HD
    scale = 1.0 / math.sqrt(HD)
    weights = w_ref[...]
    for g in range(count):
        head = (lax.axis_index("roll") ^ off) * count + g
        here = slice(g * HD, (g + 1) * HD)
        keys = jnp.concatenate([kv_ref[c, 0, :, here] for c in range(pieces)], 0)
        values = jnp.concatenate([kv_ref[c, 1, :, here] for c in range(pieces)], 0)
        places = [pl.ds(pl.multiple_of((head * per_kv + h) * HD, HD), HD) for h in range(per_kv)]
        q = jnp.concatenate([q_ref[:, c] for c in places], 0)
        go = jnp.concatenate([(ct_ref[:, c].astype(F32) * weights).astype(BF16) for c in places], 0)
        lines = pl.ds(pl.multiple_of(head * per_kv, per_kv), per_kv)
        offset = jnp.concatenate([o_ref[lines, :][h : h + 1] for h in range(per_kv)], 1)
        delta = jnp.concatenate([d_ref[lines, :][h : h + 1] for h in range(per_kv)], 1)
        scores = lax.dot_general(keys, q, NT, preferred_element_type=F32)
        prob = jnp.exp2(scores * (scale * math.log2(math.e)) - offset)
        dprob = lax.dot_general(values, go, NT, preferred_element_type=F32)
        dscore = ((prob * scale) * (dprob - delta)).astype(BF16)
        dq = lax.dot_general(dscore, keys, TN, preferred_element_type=F32).astype(BF16)
        for h in range(per_kv):
            dq_ref[:, g * span + h * HD : g * span + (h + 1) * HD] = dq[h * tokens : (h + 1) * tokens]
        dk = jnp.dot(dscore, q, preferred_element_type=F32)
        dv = jnp.dot(prob.astype(BF16), go, preferred_element_type=F32)
        for c in range(pieces):
            part = slice(c * rows, (c + 1) * rows)
            grads_ref[c, 0, :, here] = dk[part].astype(grads_ref.dtype)
            grads_ref[c, 1, :, here] = dv[part].astype(grads_ref.dtype)


def head_block(off, kv_width, queries, cotangent, weights, offset, delta, kv, out_type):
    tokens, width = queries.shape
    pieces, _, rows, cols = kv.shape
    per_kv = width // kv_width
    slab = rows * pieces
    return pl.pallas_call(
        functools.partial(heads_kernel, per_kv, off),
        in_specs=[WHOLE] * 6,
        out_specs=[WHOLE, WHOLE],
        out_shape=[
            jax.ShapeDtypeStruct((tokens, per_kv * cols), BF16),
            jax.ShapeDtypeStruct((pieces, 2, rows, cols), out_type),
        ],
        compiler_params=pltpu.CompilerParams(vmem_limit_bytes=16 * MIB + slab * 32 * 1024),
        cost_estimate=pl.CostEstimate(
            flops=30 * tokens * per_kv * slab * cols, bytes_accessed=0, transcendentals=0
        ),
        name="head_block",
    )(queries, cotangent, weights, offset, delta, kv)


def finish(order, parts, own, received):
    tokens, span = parts[0].shape
    count = len(parts)

    def kernel(*refs):
        own_ref = refs[count]
        received_refs = refs[count + 1 : -4]
        out_ref, owned_ref, total_ref, sems = refs[-4:]
        roll = lax.axis_index("roll")
        copies = [
            pltpu.make_async_copy(
                refs[i],
                out_ref.at[:, pl.ds(pl.multiple_of((roll ^ order[i]) * span, span), span)],
                sems.at[i],
            )
            for i in range(count)
        ]
        for copy in copies:
            copy.start()
        total = own_ref[...]
        for ref in received_refs:
            total = total + ref[...].astype(F32)
        total_ref[...] = total
        copies.append(pltpu.make_async_copy(total_ref, owned_ref, sems.at[count]))
        copies[-1].start()
        for copy in copies:
            copy.wait()

    anywhere = pl.BlockSpec(memory_space=pl.ANY)
    return pl.pallas_call(
        kernel,
        in_specs=[anywhere] * count + [WHOLE] * (1 + len(received)),
        out_specs=[anywhere, anywhere],
        out_shape=[
            jax.ShapeDtypeStruct((tokens, span * count), BF16),
            jax.ShapeDtypeStruct(own.shape, F32),
        ],
        scratch_shapes=[pltpu.VMEM(own.shape, F32), pltpu.SemaphoreType.DMA((count + 1,))],
        compiler_params=pltpu.CompilerParams(vmem_limit_bytes=4 * MIB),
        cost_estimate=pl.CostEstimate(flops=2**30, bytes_accessed=0, transcendentals=0),
        name="finish",
    )(*parts, own, *received)


def add(wide, narrow, out_types, apart):
    count = len(narrow)

    def kernel(wide_ref, *refs):
        for k in range(wide.shape[0]) if apart else [slice(None)]:
            total = wide_ref[k]
            for ref in refs[:count]:
                total = total + ref[k].astype(F32)
            if apart:
                refs[count + k][...] = total.astype(out_types[k])
            else:
                for ref in refs[count:]:
                    ref[...] = total.astype(ref.dtype)

    shape = wide.shape[1:] if apart else wide.shape
    return pl.pallas_call(
        kernel,
        in_specs=[WHOLE] * (1 + count),
        out_specs=[WHOLE] * len(out_types),
        out_shape=[jax.ShapeDtypeStruct(shape, t) for t in out_types],
        compiler_params=pltpu.CompilerParams(vmem_limit_bytes=16 * MIB),
        cost_estimate=pl.CostEstimate(flops=2**28, bytes_accessed=0, transcendentals=0),
        name="add_sums",
    )(wide, *narrow)


def cut(x, count, shares):
    rows, width = x.shape
    span = width // (count * shares)

    def kernel(x_ref, *refs):
        part_refs, sems = refs[:-1], refs[-1]
        ctx = lax.axis_index("ctx")
        share = lax.axis_index("roll") % shares
        copies = [
            pltpu.make_async_copy(
                x_ref.at[:, pl.ds(pl.multiple_of((shares * (ctx ^ k) + share) * span, span), span)],
                part_refs[k],
                sems.at[k],
            )
            for k in range(count)
        ]
        for copy in copies:
            copy.start()
        for copy in copies:
            copy.wait()

    anywhere = pl.BlockSpec(memory_space=pl.ANY)
    return pl.pallas_call(
        kernel,
        in_specs=[anywhere],
        out_specs=[anywhere] * count,
        out_shape=[jax.ShapeDtypeStruct((rows, span), x.dtype)] * count,
        scratch_shapes=[pltpu.SemaphoreType.DMA((count,))],
        compiler_params=pltpu.CompilerParams(vmem_limit_bytes=4 * MIB),
        cost_estimate=pl.CostEstimate(flops=2**30, bytes_accessed=0, transcendentals=0),
        name="cut_hidden",
    )(x)


def turn(x):
    count = len(x)
    rows, cols = x[0].shape

    def kernel(*refs):
        refs[count][...] = jnp.transpose(jnp.concatenate([r[...] for r in refs[:count]], 0))

    return pl.pallas_call(
        kernel,
        in_specs=[WHOLE] * count,
        out_specs=WHOLE,
        out_shape=jax.ShapeDtypeStruct((cols, rows * count), BF16),
        compiler_params=pltpu.CompilerParams(vmem_limit_bytes=12 * MIB),
        cost_estimate=pl.CostEstimate(flops=2**29, bytes_accessed=0, transcendentals=0),
        name="turn_hidden",
    )(*x)


def weight_grads(offsets, shares, low):
    total = len(offsets)
    _, span, slab = shares[0].shape
    _, rows, cols = low[0].shape
    step = min(span, 256)
    steps = span // step
    slots = [(ref, i) for ref, x in enumerate(shares) for i in range(x.shape[0])]

    def kernel(*refs):
        x_refs = refs[: len(shares)]
        low_refs = refs[len(shares) : len(shares) + len(low)]
        out_ref, tiles, sems = refs[len(shares) + len(low) :]
        keys = jnp.concatenate([r[0] for r in low_refs], 0)
        values = jnp.concatenate([r[1] for r in low_refs], 0)
        mine = lax.axis_index("roll") % total
        copies = []
        for offset, (ref, i) in zip(offsets, slots, strict=True):
            for j in range(steps):
                n = len(copies)
                x = x_refs[ref][i, j * step : (j + 1) * step]
                tiles[n, 0] = jnp.dot(x, keys, preferred_element_type=F32)
                tiles[n, 1] = jnp.dot(x, values, preferred_element_type=F32)
                row = pl.multiple_of((mine ^ offset) * span + j * step, step)
                copies.append(
                    pltpu.make_async_copy(tiles.at[n], out_ref.at[:, pl.ds(row, step), :], sems.at[n])
                )
                copies[-1].start()
        for copy in copies:
            copy.wait()

    return pl.pallas_call(
        kernel,
        in_specs=[WHOLE] * (len(shares) + len(low)),
        out_specs=pl.BlockSpec(memory_space=pl.ANY),
        out_shape=jax.ShapeDtypeStruct((2, total * span, cols), F32),
        scratch_shapes=[
            pltpu.VMEM((total * steps, 2, step, cols), F32),
            pltpu.SemaphoreType.DMA((total * steps,)),
        ],
        compiler_params=pltpu.CompilerParams(vmem_limit_bytes=24 * MIB),
        cost_estimate=pl.CostEstimate(flops=2**31, bytes_accessed=0, transcendentals=0),
        name="weight_grads",
    )(*shares, *low)


def on_device(
    queries,
    cotangent,
    out_dot,
    norm_offset,
    prompt_kv,
    prompt_x,
    block_ids,
    lengths,
    advantages,
    adv_index,
):
    ctx_count = lax.axis_size("ctx")
    roll_count = lax.axis_size("roll")
    roll = lax.axis_index("roll")
    _, rows, kv_width = prompt_kv.shape
    cols = kv_width // roll_count
    slab = rows * ctx_count

    def to_ctx(x, offset):
        return lax.ppermute(x, "ctx", xor_pairs(ctx_count, offset))

    def to_roll(x, offset):
        return lax.ppermute(x, "roll", xor_pairs(roll_count, offset))

    last = roll_count - 1
    own = lax.dynamic_slice_in_dim(prompt_kv, (roll ^ last) * cols, cols, 2)
    fetched = jnp.stack([own] + [to_ctx(own, k) for k in range(1, ctx_count)])
    blocks = {last: fetched, last - 1: to_roll(fetched, 1)}
    for d in range(1, roll_count // 2):
        blocks[last - 2 * d] = to_roll(fetched, 2 * d)
        blocks[last - 2 * d - 1] = to_roll(blocks[last - 2 * d], 1)

    shares = roll_count
    while prompt_x.shape[1] // (ctx_count * shares) % HD:
        shares //= 2
    x_cut = cut(prompt_x, ctx_count, shares)
    out_dot, x_cut = lax.optimization_barrier((out_dot, x_cut))
    x_share = turn([x_cut[0]] + [to_ctx(x_cut[k], k) for k in range(1, ctx_count)])[None]

    blocks_total = block_ids.shape[0] * ctx_count * roll_count
    weights, delta, offset = prep(
        blocks_total // lengths.shape[0], slab, block_ids, lengths, advantages, adv_index, out_dot.T, norm_offset.T
    )

    order = list(reversed(range(roll_count)))
    dq = []
    arrived = []
    for off in order:
        kind = BF16 if off % 2 else F32
        part, grads = head_block(
            off, kv_width, queries, cotangent, weights, offset, delta, blocks[off], kind
        )
        dq.append(part)
        if off % 2:
            sibling = to_roll(grads, 1)
        elif off:
            (total,) = add(grads, [sibling], [BF16], False)
            delta, total = lax.optimization_barrier((delta, total))
            arrived.append(to_roll(total, off))
    sums = list(add(grads, [sibling] + arrived, [F32] + [BF16] * (ctx_count - 1), True))
    received = [to_ctx(sums[k], k) for k in range(1, ctx_count)]

    (owned_low,) = add(sums[0], received, [BF16], False)
    offsets, x_parts = [0], [x_share]
    bit = shares // 2
    while bit:
        whole = x_parts[0] if len(x_parts) == 1 else jnp.concatenate(x_parts)
        x_parts.append(to_roll(whole, bit))
        offsets += [offset ^ bit for offset in offsets]
        bit //= 2
        if bit:
            x_parts[-1] = lax.optimization_barrier((x_parts[-1], owned_low))[0]
    low = [owned_low] + [to_ctx(owned_low, k) for k in range(1, ctx_count)]
    dq, sums[0], owned_low = lax.optimization_barrier((dq, sums[0], owned_low))
    query_grad, owned = finish(order, dq, sums[0], received)
    return (query_grad, owned, weight_grads(offsets, x_parts, low))


def solution(mesh):
    placed = (
        P(("groups", "ctx", "roll"), None),
        P(("groups", "ctx", "roll"), None),
        P(("groups", "ctx", "roll"), None),
        P(("groups", "ctx", "roll"), None),
        P(None, ("groups", "ctx"), None),
        P(("groups", "ctx"), None),
        P(("groups", "ctx", "roll")),
        P("groups"),
        P("groups"),
        P("groups"),
    )
    return jax.shard_map(
        on_device,
        mesh=mesh,
        in_specs=placed,
        out_specs=(
            P(("groups", "ctx", "roll"), None),
            P(None, ("groups", "ctx"), "roll"),
            P(None, ("groups", "ctx"), "roll"),
        ),
        check_vma=False,
    )
```

```python
import functools
import math

import jax
import jax.numpy as jnp
from jax import lax
from jax.experimental import pallas as pl
from jax.experimental.pallas import tpu as pltpu
from jax.sharding import PartitionSpec as P

HD = 128
BLOCK = 32
MIB = 2**20
NT = (((1,), (1,)), ((), ()))
TN = (((0,), (0,)), ((), ()))
F32 = jnp.float32
BF16 = jnp.bfloat16
WHOLE = pl.BlockSpec(memory_space=pltpu.VMEM)


def xor_pairs(count, offset):
    return [(i, i ^ offset) for i in range(count)]


def prep_kernel(per_rollout, slab, ids, lengths, advantages, adv_index, od_ref, no_ref, w_ref, d_ref, o_ref):
    resp_max = per_rollout * BLOCK
    rows = []
    for b in range(ids.shape[0]):
        rollout = ids[b] // per_rollout
        slot = ids[b] % per_rollout
        length = lengths[rollout]
        scaled = jnp.full((BLOCK, HD), advantages[adv_index[rollout]] * resp_max, F32) / jnp.full(
            (BLOCK, HD), length.astype(F32), F32
        )
        position = slot * BLOCK + lax.broadcasted_iota(jnp.int32, (BLOCK, HD), 0)
        rows.append(jnp.where(position < length, scaled, jnp.float32(0.0)))
    weights = jnp.concatenate(rows, 0)
    w_ref[...] = weights
    d_ref[...] = jnp.transpose(weights)[: od_ref.shape[0]] * od_ref[...]
    o_ref[...] = no_ref[...] * math.log2(math.e) + math.log2(slab)


def prep(per_rollout, slab, ids, lengths, advantages, adv_index, out_dot, norm_offset):
    heads, tokens = out_dot.shape
    scalars = pl.BlockSpec(memory_space=pltpu.SMEM)
    return pl.pallas_call(
        functools.partial(prep_kernel, per_rollout, slab),
        in_specs=[scalars] * 4 + [WHOLE] * 2,
        out_specs=[WHOLE] * 3,
        out_shape=[
            jax.ShapeDtypeStruct((tokens, HD), F32),
            jax.ShapeDtypeStruct((heads, tokens), F32),
            jax.ShapeDtypeStruct((heads, tokens), F32),
        ],
        compiler_params=pltpu.CompilerParams(vmem_limit_bytes=4 * MIB),
        cost_estimate=pl.CostEstimate(flops=2**30, bytes_accessed=0, transcendentals=0),
        name="prep",
    )(ids, lengths, advantages, adv_index, out_dot, norm_offset)


def heads_kernel(per_kv, off, q_ref, ct_ref, w_ref, o_ref, d_ref, kv_ref, dq_ref, grads_ref):
    tokens = q_ref.shape[0]
    pieces, _, rows, cols = kv_ref.shape
    count = cols // HD
    span = per_kv * HD
    scale = 1.0 / math.sqrt(HD)
    weights = w_ref[...]
    for g in range(count):
        head = (lax.axis_index("roll") ^ off) * count + g
        here = slice(g * HD, (g + 1) * HD)
        keys = jnp.concatenate([kv_ref[c, 0, :, here] for c in range(pieces)], 0)
        values = jnp.concatenate([kv_ref[c, 1, :, here] for c in range(pieces)], 0)
        places = [pl.ds(pl.multiple_of((head * per_kv + h) * HD, HD), HD) for h in range(per_kv)]
        q = jnp.concatenate([q_ref[:, c] for c in places], 0)
        go = jnp.concatenate([(ct_ref[:, c].astype(F32) * weights).astype(BF16) for c in places], 0)
        lines = pl.ds(pl.multiple_of(head * per_kv, per_kv), per_kv)
        offset = jnp.concatenate([o_ref[lines, :][h : h + 1] for h in range(per_kv)], 1)
        delta = jnp.concatenate([d_ref[lines, :][h : h + 1] for h in range(per_kv)], 1)
        scores = lax.dot_general(keys, q, NT, preferred_element_type=F32)
        prob = jnp.exp2(scores * (scale * math.log2(math.e)) - offset)
        dprob = lax.dot_general(values, go, NT, preferred_element_type=F32)
        dscore = ((prob * scale) * (dprob - delta)).astype(BF16)
        dq = lax.dot_general(dscore, keys, TN, preferred_element_type=F32).astype(BF16)
        for h in range(per_kv):
            dq_ref[:, g * span + h * HD : g * span + (h + 1) * HD] = dq[h * tokens : (h + 1) * tokens]
        dk = jnp.dot(dscore, q, preferred_element_type=F32)
        dv = jnp.dot(prob.astype(BF16), go, preferred_element_type=F32)
        for c in range(pieces):
            part = slice(c * rows, (c + 1) * rows)
            grads_ref[c, 0, :, here] = dk[part].astype(grads_ref.dtype)
            grads_ref[c, 1, :, here] = dv[part].astype(grads_ref.dtype)


def head_block(off, kv_width, queries, cotangent, weights, offset, delta, kv, out_type):
    tokens, width = queries.shape
    pieces, _, rows, cols = kv.shape
    per_kv = width // kv_width
    slab = rows * pieces
    return pl.pallas_call(
        functools.partial(heads_kernel, per_kv, off),
        in_specs=[WHOLE] * 6,
        out_specs=[WHOLE, WHOLE],
        out_shape=[
            jax.ShapeDtypeStruct((tokens, per_kv * cols), BF16),
            jax.ShapeDtypeStruct((pieces, 2, rows, cols), out_type),
        ],
        compiler_params=pltpu.CompilerParams(vmem_limit_bytes=16 * MIB + slab * 32 * 1024),
        cost_estimate=pl.CostEstimate(
            flops=30 * tokens * per_kv * slab * cols, bytes_accessed=0, transcendentals=0
        ),
        name="head_block",
    )(queries, cotangent, weights, offset, delta, kv)


def finish(order, parts, own, received):
    tokens, span = parts[0].shape
    count = len(parts)

    def kernel(*refs):
        own_ref = refs[count]
        received_refs = refs[count + 1 : -4]
        out_ref, owned_ref, total_ref, sems = refs[-4:]
        roll = lax.axis_index("roll")
        copies = [
            pltpu.make_async_copy(
                refs[i],
                out_ref.at[:, pl.ds(pl.multiple_of((roll ^ order[i]) * span, span), span)],
                sems.at[i],
            )
            for i in range(count)
        ]
        for copy in copies:
            copy.start()
        total = own_ref[...]
        for ref in received_refs:
            total = total + ref[...].astype(F32)
        total_ref[...] = total
        copies.append(pltpu.make_async_copy(total_ref, owned_ref, sems.at[count]))
        copies[-1].start()
        for copy in copies:
            copy.wait()

    anywhere = pl.BlockSpec(memory_space=pl.ANY)
    return pl.pallas_call(
        kernel,
        in_specs=[anywhere] * count + [WHOLE] * (1 + len(received)),
        out_specs=[anywhere, anywhere],
        out_shape=[
            jax.ShapeDtypeStruct((tokens, span * count), BF16),
            jax.ShapeDtypeStruct(own.shape, F32),
        ],
        scratch_shapes=[pltpu.VMEM(own.shape, F32), pltpu.SemaphoreType.DMA((count + 1,))],
        compiler_params=pltpu.CompilerParams(vmem_limit_bytes=4 * MIB),
        cost_estimate=pl.CostEstimate(flops=2**30, bytes_accessed=0, transcendentals=0),
        name="finish",
    )(*parts, own, *received)


def add(wide, narrow, out_types, apart):
    count = len(narrow)

    def kernel(wide_ref, *refs):
        for k in range(wide.shape[0]) if apart else [slice(None)]:
            total = wide_ref[k]
            for ref in refs[:count]:
                total = total + ref[k].astype(F32)
            if apart:
                refs[count + k][...] = total.astype(out_types[k])
            else:
                for ref in refs[count:]:
                    ref[...] = total.astype(ref.dtype)

    shape = wide.shape[1:] if apart else wide.shape
    return pl.pallas_call(
        kernel,
        in_specs=[WHOLE] * (1 + count),
        out_specs=[WHOLE] * len(out_types),
        out_shape=[jax.ShapeDtypeStruct(shape, t) for t in out_types],
        compiler_params=pltpu.CompilerParams(vmem_limit_bytes=16 * MIB),
        cost_estimate=pl.CostEstimate(flops=2**28, bytes_accessed=0, transcendentals=0),
        name="add_sums",
    )(wide, *narrow)


def cut(x, count, shares):
    rows, width = x.shape
    span = width // (count * shares)

    def kernel(x_ref, *refs):
        part_refs, sems = refs[:-1], refs[-1]
        ctx = lax.axis_index("ctx")
        share = lax.axis_index("roll") % shares
        copies = [
            pltpu.make_async_copy(
                x_ref.at[:, pl.ds(pl.multiple_of((shares * (ctx ^ k) + share) * span, span), span)],
                part_refs[k],
                sems.at[k],
            )
            for k in range(count)
        ]
        for copy in copies:
            copy.start()
        for copy in copies:
            copy.wait()

    anywhere = pl.BlockSpec(memory_space=pl.ANY)
    return pl.pallas_call(
        kernel,
        in_specs=[anywhere],
        out_specs=[anywhere] * count,
        out_shape=[jax.ShapeDtypeStruct((rows, span), x.dtype)] * count,
        scratch_shapes=[pltpu.SemaphoreType.DMA((count,))],
        compiler_params=pltpu.CompilerParams(vmem_limit_bytes=4 * MIB),
        cost_estimate=pl.CostEstimate(flops=2**30, bytes_accessed=0, transcendentals=0),
        name="cut_hidden",
    )(x)


def turn(x):
    count = len(x)
    rows, cols = x[0].shape

    def kernel(*refs):
        refs[count][...] = jnp.transpose(jnp.concatenate([r[...] for r in refs[:count]], 0))

    return pl.pallas_call(
        kernel,
        in_specs=[WHOLE] * count,
        out_specs=WHOLE,
        out_shape=jax.ShapeDtypeStruct((cols, rows * count), BF16),
        compiler_params=pltpu.CompilerParams(vmem_limit_bytes=12 * MIB),
        cost_estimate=pl.CostEstimate(flops=2**29, bytes_accessed=0, transcendentals=0),
        name="turn_hidden",
    )(*x)


def weight_grads(offsets, shares, low):
    total = len(offsets)
    _, span, slab = shares[0].shape
    _, rows, cols = low[0].shape
    step = min(span, 512)
    steps = span // step
    slots = [(ref, i) for ref, x in enumerate(shares) for i in range(x.shape[0])]

    def kernel(*refs):
        x_refs = refs[: len(shares)]
        low_refs = refs[len(shares) : len(shares) + len(low)]
        out_ref, tiles, sems = refs[len(shares) + len(low) :]
        keys = jnp.concatenate([r[0] for r in low_refs], 0)
        values = jnp.concatenate([r[1] for r in low_refs], 0)
        mine = lax.axis_index("roll") % total
        copies = []
        for offset, (ref, i) in zip(offsets, slots, strict=True):
            for j in range(steps):
                n = len(copies)
                x = x_refs[ref][i, j * step : (j + 1) * step]
                tiles[n, 0] = jnp.dot(x, keys, preferred_element_type=F32)
                tiles[n, 1] = jnp.dot(x, values, preferred_element_type=F32)
                row = pl.multiple_of((mine ^ offset) * span + j * step, step)
                copies.append(
                    pltpu.make_async_copy(tiles.at[n], out_ref.at[:, pl.ds(row, step), :], sems.at[n])
                )
                copies[-1].start()
        for copy in copies:
            copy.wait()

    return pl.pallas_call(
        kernel,
        in_specs=[WHOLE] * (len(shares) + len(low)),
        out_specs=pl.BlockSpec(memory_space=pl.ANY),
        out_shape=jax.ShapeDtypeStruct((2, total * span, cols), F32),
        scratch_shapes=[
            pltpu.VMEM((total * steps, 2, step, cols), F32),
            pltpu.SemaphoreType.DMA((total * steps,)),
        ],
        compiler_params=pltpu.CompilerParams(vmem_limit_bytes=24 * MIB),
        cost_estimate=pl.CostEstimate(flops=2**31, bytes_accessed=0, transcendentals=0),
        name="weight_grads",
    )(*shares, *low)


def on_device(
    queries,
    cotangent,
    out_dot,
    norm_offset,
    prompt_kv,
    prompt_x,
    block_ids,
    lengths,
    advantages,
    adv_index,
):
    ctx_count = lax.axis_size("ctx")
    roll_count = lax.axis_size("roll")
    roll = lax.axis_index("roll")
    _, rows, kv_width = prompt_kv.shape
    cols = kv_width // roll_count
    slab = rows * ctx_count

    def to_ctx(x, offset):
        return lax.ppermute(x, "ctx", xor_pairs(ctx_count, offset))

    def to_roll(x, offset):
        return lax.ppermute(x, "roll", xor_pairs(roll_count, offset))

    last = roll_count - 1
    own = lax.dynamic_slice_in_dim(prompt_kv, (roll ^ last) * cols, cols, 2)
    fetched = jnp.stack([own] + [to_ctx(own, k) for k in range(1, ctx_count)])
    blocks = {last: fetched, last - 1: to_roll(fetched, 1)}
    for d in range(1, roll_count // 2):
        blocks[last - 2 * d] = to_roll(fetched, 2 * d)
        blocks[last - 2 * d - 1] = to_roll(blocks[last - 2 * d], 1)

    shares = roll_count
    while prompt_x.shape[1] // (ctx_count * shares) % HD:
        shares //= 2
    x_cut = cut(prompt_x, ctx_count, shares)
    out_dot, x_cut = lax.optimization_barrier((out_dot, x_cut))
    x_pieces = [x_cut[0]] + [to_ctx(x_cut[k], k) for k in range(1, ctx_count)]

    blocks_total = block_ids.shape[0] * ctx_count * roll_count
    weights, delta, offset = prep(
        blocks_total // lengths.shape[0], slab, block_ids, lengths, advantages, adv_index, out_dot.T, norm_offset.T
    )

    order = list(reversed(range(roll_count)))
    dq = []
    arrived = []
    for off in order:
        kind = BF16 if off % 2 else F32
        part, grads = head_block(
            off, kv_width, queries, cotangent, weights, offset, delta, blocks[off], kind
        )
        dq.append(part)
        if off == 1:
            x_pieces = lax.optimization_barrier((x_pieces, grads))[0]
            x_share = turn(x_pieces)[None]
        if off % 2:
            sibling = to_roll(grads, 1)
        elif off:
            (total,) = add(grads, [sibling], [BF16], False)
            delta, total = lax.optimization_barrier((delta, total))
            arrived.append(to_roll(total, off))
    sums = list(add(grads, [sibling] + arrived, [F32] + [BF16] * (ctx_count - 1), True))
    received = [to_ctx(sums[k], k) for k in range(1, ctx_count)]

    (owned_low,) = add(sums[0], received, [BF16], False)
    x_share = lax.optimization_barrier((x_share, sums[0]))[0]
    offsets, x_parts = [0], [x_share]
    bit = shares // 2
    while bit:
        whole = x_parts[0] if len(x_parts) == 1 else jnp.concatenate(x_parts)
        x_parts.append(to_roll(whole, bit))
        offsets += [offset ^ bit for offset in offsets]
        bit //= 2
        if bit:
            x_parts[-1] = lax.optimization_barrier((x_parts[-1], owned_low))[0]
    low = [owned_low] + [to_ctx(owned_low, k) for k in range(1, ctx_count)]
    dq, sums[0], owned_low = lax.optimization_barrier((dq, sums[0], owned_low))
    query_grad, owned = finish(order, dq, sums[0], received)
    return (query_grad, owned, weight_grads(offsets, x_parts, low))


def solution(mesh):
    placed = (
        P(("groups", "ctx", "roll"), None),
        P(("groups", "ctx", "roll"), None),
        P(("groups", "ctx", "roll"), None),
        P(("groups", "ctx", "roll"), None),
        P(None, ("groups", "ctx"), None),
        P(("groups", "ctx"), None),
        P(("groups", "ctx", "roll")),
        P("groups"),
        P("groups"),
        P("groups"),
    )
    return jax.shard_map(
        on_device,
        mesh=mesh,
        in_specs=placed,
        out_specs=(
            P(("groups", "ctx", "roll"), None),
            P(None, ("groups", "ctx"), "roll"),
            P(None, ("groups", "ctx"), "roll"),
        ),
        check_vma=False,
    )
```

```python
import functools
import math

import jax
import jax.numpy as jnp
from jax import lax
from jax.experimental import pallas as pl
from jax.experimental.pallas import tpu as pltpu
from jax.sharding import PartitionSpec as P

HD = 128
BLOCK = 32
MIB = 2**20
NT = (((1,), (1,)), ((), ()))
TN = (((0,), (0,)), ((), ()))
F32 = jnp.float32
BF16 = jnp.bfloat16
WHOLE = pl.BlockSpec(memory_space=pltpu.VMEM)


def xor_pairs(count, offset):
    return [(i, i ^ offset) for i in range(count)]


def prep_kernel(per_rollout, slab, ids, lengths, advantages, adv_index, od_ref, no_ref, w_ref, d_ref, o_ref):
    resp_max = per_rollout * BLOCK
    rows = []
    for b in range(ids.shape[0]):
        rollout = ids[b] // per_rollout
        slot = ids[b] % per_rollout
        length = lengths[rollout]
        scaled = jnp.full((BLOCK, HD), advantages[adv_index[rollout]] * resp_max, F32) / jnp.full(
            (BLOCK, HD), length.astype(F32), F32
        )
        position = slot * BLOCK + lax.broadcasted_iota(jnp.int32, (BLOCK, HD), 0)
        rows.append(jnp.where(position < length, scaled, jnp.float32(0.0)))
    weights = jnp.concatenate(rows, 0)
    w_ref[...] = weights
    d_ref[...] = jnp.transpose(weights)[: od_ref.shape[0]] * od_ref[...]
    o_ref[...] = no_ref[...] * math.log2(math.e) + math.log2(slab)


def prep(per_rollout, slab, ids, lengths, advantages, adv_index, out_dot, norm_offset):
    heads, tokens = out_dot.shape
    scalars = pl.BlockSpec(memory_space=pltpu.SMEM)
    return pl.pallas_call(
        functools.partial(prep_kernel, per_rollout, slab),
        in_specs=[scalars] * 4 + [WHOLE] * 2,
        out_specs=[WHOLE] * 3,
        out_shape=[
            jax.ShapeDtypeStruct((tokens, HD), F32),
            jax.ShapeDtypeStruct((heads, tokens), F32),
            jax.ShapeDtypeStruct((heads, tokens), F32),
        ],
        compiler_params=pltpu.CompilerParams(vmem_limit_bytes=4 * MIB),
        cost_estimate=pl.CostEstimate(flops=2**30, bytes_accessed=0, transcendentals=0),
        name="prep",
    )(ids, lengths, advantages, adv_index, out_dot, norm_offset)


def heads_kernel(per_kv, off, q_ref, ct_ref, w_ref, o_ref, d_ref, kv_ref, dq_ref, grads_ref):
    tokens = q_ref.shape[0]
    pieces, _, rows, cols = kv_ref.shape
    count = cols // HD
    span = per_kv * HD
    scale = 1.0 / math.sqrt(HD)
    weights = w_ref[...]
    for g in range(count):
        head = (lax.axis_index("roll") ^ off) * count + g
        here = slice(g * HD, (g + 1) * HD)
        keys = jnp.concatenate([kv_ref[c, 0, :, here] for c in range(pieces)], 0)
        values = jnp.concatenate([kv_ref[c, 1, :, here] for c in range(pieces)], 0)
        places = [pl.ds(pl.multiple_of((head * per_kv + h) * HD, HD), HD) for h in range(per_kv)]
        q = jnp.concatenate([q_ref[:, c] for c in places], 0)
        go = jnp.concatenate([(ct_ref[:, c].astype(F32) * weights).astype(BF16) for c in places], 0)
        lines = pl.ds(pl.multiple_of(head * per_kv, per_kv), per_kv)
        offset = jnp.concatenate([o_ref[lines, :][h : h + 1] for h in range(per_kv)], 1)
        delta = jnp.concatenate([d_ref[lines, :][h : h + 1] for h in range(per_kv)], 1)
        scores = lax.dot_general(keys, q, NT, preferred_element_type=F32)
        prob = jnp.exp2(scores * (scale * math.log2(math.e)) - offset)
        dprob = lax.dot_general(values, go, NT, preferred_element_type=F32)
        dscore = ((prob * scale) * (dprob - delta)).astype(BF16)
        dq = lax.dot_general(dscore, keys, TN, preferred_element_type=F32).astype(BF16)
        for h in range(per_kv):
            dq_ref[:, g * span + h * HD : g * span + (h + 1) * HD] = dq[h * tokens : (h + 1) * tokens]
        dk = jnp.dot(dscore, q, preferred_element_type=F32)
        dv = jnp.dot(prob.astype(BF16), go, preferred_element_type=F32)
        for c in range(pieces):
            part = slice(c * rows, (c + 1) * rows)
            grads_ref[c, 0, :, here] = dk[part].astype(grads_ref.dtype)
            grads_ref[c, 1, :, here] = dv[part].astype(grads_ref.dtype)


def head_block(off, kv_width, queries, cotangent, weights, offset, delta, kv, out_type):
    tokens, width = queries.shape
    pieces, _, rows, cols = kv.shape
    per_kv = width // kv_width
    slab = rows * pieces
    return pl.pallas_call(
        functools.partial(heads_kernel, per_kv, off),
        in_specs=[WHOLE] * 6,
        out_specs=[WHOLE, WHOLE],
        out_shape=[
            jax.ShapeDtypeStruct((tokens, per_kv * cols), BF16),
            jax.ShapeDtypeStruct((pieces, 2, rows, cols), out_type),
        ],
        compiler_params=pltpu.CompilerParams(vmem_limit_bytes=16 * MIB + slab * 32 * 1024),
        cost_estimate=pl.CostEstimate(
            flops=80 * tokens * per_kv * slab * cols, bytes_accessed=0, transcendentals=0
        ),
        name="head_block",
    )(queries, cotangent, weights, offset, delta, kv)


def finish(order, parts, own, received):
    tokens, span = parts[0].shape
    count = len(parts)

    def kernel(*refs):
        own_ref = refs[count]
        received_refs = refs[count + 1 : -4]
        out_ref, owned_ref, total_ref, sems = refs[-4:]
        roll = lax.axis_index("roll")
        copies = [
            pltpu.make_async_copy(
                refs[i],
                out_ref.at[:, pl.ds(pl.multiple_of((roll ^ order[i]) * span, span), span)],
                sems.at[i],
            )
            for i in range(count)
        ]
        for copy in copies:
            copy.start()
        total = own_ref[...]
        for ref in received_refs:
            total = total + ref[...].astype(F32)
        total_ref[...] = total
        copies.append(pltpu.make_async_copy(total_ref, owned_ref, sems.at[count]))
        copies[-1].start()
        for copy in copies:
            copy.wait()

    anywhere = pl.BlockSpec(memory_space=pl.ANY)
    return pl.pallas_call(
        kernel,
        in_specs=[anywhere] * count + [WHOLE] * (1 + len(received)),
        out_specs=[anywhere, anywhere],
        out_shape=[
            jax.ShapeDtypeStruct((tokens, span * count), BF16),
            jax.ShapeDtypeStruct(own.shape, F32),
        ],
        scratch_shapes=[pltpu.VMEM(own.shape, F32), pltpu.SemaphoreType.DMA((count + 1,))],
        compiler_params=pltpu.CompilerParams(vmem_limit_bytes=4 * MIB),
        cost_estimate=pl.CostEstimate(flops=2**30, bytes_accessed=0, transcendentals=0),
        name="finish",
    )(*parts, own, *received)


def add(wide, narrow, out_types, apart):
    count = len(narrow)

    def kernel(wide_ref, *refs):
        for k in range(wide.shape[0]) if apart else [slice(None)]:
            total = wide_ref[k]
            for ref in refs[:count]:
                total = total + ref[k].astype(F32)
            if apart:
                refs[count + k][...] = total.astype(out_types[k])
            else:
                for ref in refs[count:]:
                    ref[...] = total.astype(ref.dtype)

    shape = wide.shape[1:] if apart else wide.shape
    return pl.pallas_call(
        kernel,
        in_specs=[WHOLE] * (1 + count),
        out_specs=[WHOLE] * len(out_types),
        out_shape=[jax.ShapeDtypeStruct(shape, t) for t in out_types],
        compiler_params=pltpu.CompilerParams(vmem_limit_bytes=16 * MIB),
        cost_estimate=pl.CostEstimate(flops=2**28, bytes_accessed=0, transcendentals=0),
        name="add_sums",
    )(wide, *narrow)


def cut(x, count, shares):
    rows, width = x.shape
    span = width // (count * shares)

    def kernel(x_ref, *refs):
        part_refs, sems = refs[:-1], refs[-1]
        ctx = lax.axis_index("ctx")
        share = lax.axis_index("roll") % shares
        copies = [
            pltpu.make_async_copy(
                x_ref.at[:, pl.ds(pl.multiple_of((shares * (ctx ^ k) + share) * span, span), span)],
                part_refs[k],
                sems.at[k],
            )
            for k in range(count)
        ]
        for copy in copies:
            copy.start()
        for copy in copies:
            copy.wait()

    anywhere = pl.BlockSpec(memory_space=pl.ANY)
    return pl.pallas_call(
        kernel,
        in_specs=[anywhere],
        out_specs=[anywhere] * count,
        out_shape=[jax.ShapeDtypeStruct((rows, span), x.dtype)] * count,
        scratch_shapes=[pltpu.SemaphoreType.DMA((count,))],
        compiler_params=pltpu.CompilerParams(vmem_limit_bytes=4 * MIB),
        cost_estimate=pl.CostEstimate(flops=2**30, bytes_accessed=0, transcendentals=0),
        name="cut_hidden",
    )(x)


def turn(x):
    count = len(x)
    rows, cols = x[0].shape

    def kernel(*refs):
        refs[count][...] = jnp.transpose(jnp.concatenate([r[...] for r in refs[:count]], 0))

    return pl.pallas_call(
        kernel,
        in_specs=[WHOLE] * count,
        out_specs=WHOLE,
        out_shape=jax.ShapeDtypeStruct((cols, rows * count), BF16),
        compiler_params=pltpu.CompilerParams(vmem_limit_bytes=12 * MIB),
        cost_estimate=pl.CostEstimate(flops=2**29, bytes_accessed=0, transcendentals=0),
        name="turn_hidden",
    )(*x)


def weight_grads(offsets, shares, low):
    total = len(offsets)
    _, span, slab = shares[0].shape
    _, rows, cols = low[0].shape
    step = min(span, 512)
    steps = span // step
    slots = [(ref, i) for ref, x in enumerate(shares) for i in range(x.shape[0])]

    def kernel(*refs):
        x_refs = refs[: len(shares)]
        low_refs = refs[len(shares) : len(shares) + len(low)]
        out_ref, tiles, sems = refs[len(shares) + len(low) :]
        keys = jnp.concatenate([r[0] for r in low_refs], 0)
        values = jnp.concatenate([r[1] for r in low_refs], 0)
        mine = lax.axis_index("roll") % total
        copies = []
        for offset, (ref, i) in zip(offsets, slots, strict=True):
            for j in range(steps):
                n = len(copies)
                x = x_refs[ref][i, j * step : (j + 1) * step]
                tiles[n, 0] = jnp.dot(x, keys, preferred_element_type=F32)
                tiles[n, 1] = jnp.dot(x, values, preferred_element_type=F32)
                row = pl.multiple_of((mine ^ offset) * span + j * step, step)
                copies.append(
                    pltpu.make_async_copy(tiles.at[n], out_ref.at[:, pl.ds(row, step), :], sems.at[n])
                )
                copies[-1].start()
        for copy in copies:
            copy.wait()

    return pl.pallas_call(
        kernel,
        in_specs=[WHOLE] * (len(shares) + len(low)),
        out_specs=pl.BlockSpec(memory_space=pl.ANY),
        out_shape=jax.ShapeDtypeStruct((2, total * span, cols), F32),
        scratch_shapes=[
            pltpu.VMEM((total * steps, 2, step, cols), F32),
            pltpu.SemaphoreType.DMA((total * steps,)),
        ],
        compiler_params=pltpu.CompilerParams(vmem_limit_bytes=24 * MIB),
        cost_estimate=pl.CostEstimate(flops=2**31, bytes_accessed=0, transcendentals=0),
        name="weight_grads",
    )(*shares, *low)


def on_device(
    queries,
    cotangent,
    out_dot,
    norm_offset,
    prompt_kv,
    prompt_x,
    block_ids,
    lengths,
    advantages,
    adv_index,
):
    ctx_count = lax.axis_size("ctx")
    roll_count = lax.axis_size("roll")
    roll = lax.axis_index("roll")
    _, rows, kv_width = prompt_kv.shape
    cols = kv_width // roll_count
    slab = rows * ctx_count

    def to_ctx(x, offset):
        return lax.ppermute(x, "ctx", xor_pairs(ctx_count, offset))

    def to_roll(x, offset):
        return lax.ppermute(x, "roll", xor_pairs(roll_count, offset))

    last = roll_count - 1
    own = lax.dynamic_slice_in_dim(prompt_kv, (roll ^ last) * cols, cols, 2)
    fetched = jnp.stack([own] + [to_ctx(own, k) for k in range(1, ctx_count)])
    blocks = {last: fetched, last - 1: to_roll(fetched, 1)}
    for d in range(1, roll_count // 2):
        blocks[last - 2 * d] = to_roll(fetched, 2 * d)
        blocks[last - 2 * d - 1] = to_roll(blocks[last - 2 * d], 1)

    shares = roll_count
    while prompt_x.shape[1] // (ctx_count * shares) % HD:
        shares //= 2
    x_cut = cut(prompt_x, ctx_count, shares)
    out_dot, x_cut = lax.optimization_barrier((out_dot, x_cut))
    x_pieces = [x_cut[0]] + [to_ctx(x_cut[k], k) for k in range(1, ctx_count)]

    blocks_total = block_ids.shape[0] * ctx_count * roll_count
    weights, delta, offset = prep(
        blocks_total // lengths.shape[0], slab, block_ids, lengths, advantages, adv_index, out_dot.T, norm_offset.T
    )

    order = list(reversed(range(roll_count)))
    dq = []
    arrived = []
    for off in order:
        kind = BF16 if off % 2 else F32
        part, grads = head_block(
            off, kv_width, queries, cotangent, weights, offset, delta, blocks[off], kind
        )
        dq.append(part)
        if off == 1:
            x_pieces = lax.optimization_barrier((x_pieces, grads))[0]
            x_share = turn(x_pieces)[None]
        if off % 2:
            sibling = to_roll(grads, 1)
        elif off:
            (total,) = add(grads, [sibling], [BF16], False)
            delta, total = lax.optimization_barrier((delta, total))
            arrived.append(to_roll(total, off))
    sums = list(add(grads, [sibling] + arrived, [F32] + [BF16] * (ctx_count - 1), True))
    received = [to_ctx(sums[k], k) for k in range(1, ctx_count)]

    (owned_low,) = add(sums[0], received, [BF16], False)
    x_share = lax.optimization_barrier((x_share, sums[0]))[0]
    offsets, x_parts = [0], [x_share]
    bit = shares // 2
    while bit:
        whole = x_parts[0] if len(x_parts) == 1 else jnp.concatenate(x_parts)
        x_parts.append(to_roll(whole, bit))
        offsets += [offset ^ bit for offset in offsets]
        bit //= 2
        if bit:
            x_parts[-1] = lax.optimization_barrier((x_parts[-1], owned_low))[0]
    low = [owned_low] + [to_ctx(owned_low, k) for k in range(1, ctx_count)]
    dq, sums[0], owned_low = lax.optimization_barrier((dq, sums[0], owned_low))
    query_grad, owned = finish(order, dq, sums[0], received)
    return (query_grad, owned, weight_grads(offsets, x_parts, low))


def solution(mesh):
    placed = (
        P(("groups", "ctx", "roll"), None),
        P(("groups", "ctx", "roll"), None),
        P(("groups", "ctx", "roll"), None),
        P(("groups", "ctx", "roll"), None),
        P(None, ("groups", "ctx"), None),
        P(("groups", "ctx"), None),
        P(("groups", "ctx", "roll")),
        P("groups"),
        P("groups"),
        P("groups"),
    )
    return jax.shard_map(
        on_device,
        mesh=mesh,
        in_specs=placed,
        out_specs=(
            P(("groups", "ctx", "roll"), None),
            P(None, ("groups", "ctx"), "roll"),
            P(None, ("groups", "ctx"), "roll"),
        ),
        check_vma=False,
    )
```

```python
import functools
import math

import jax
import jax.numpy as jnp
from jax import lax
from jax.experimental import pallas as pl
from jax.experimental.pallas import tpu as pltpu
from jax.sharding import PartitionSpec as P

HD = 128
BLOCK = 32
MIB = 2**20
NT = (((1,), (1,)), ((), ()))
TN = (((0,), (0,)), ((), ()))
F32 = jnp.float32
BF16 = jnp.bfloat16
WHOLE = pl.BlockSpec(memory_space=pltpu.VMEM)


def xor_pairs(count, offset):
    return [(i, i ^ offset) for i in range(count)]


def prep_kernel(per_rollout, slab, ids, lengths, advantages, adv_index, od_ref, no_ref, w_ref, d_ref, o_ref):
    resp_max = per_rollout * BLOCK
    rows = []
    for b in range(ids.shape[0]):
        rollout = ids[b] // per_rollout
        slot = ids[b] % per_rollout
        length = lengths[rollout]
        scaled = jnp.full((BLOCK, HD), advantages[adv_index[rollout]] * resp_max, F32) / jnp.full(
            (BLOCK, HD), length.astype(F32), F32
        )
        position = slot * BLOCK + lax.broadcasted_iota(jnp.int32, (BLOCK, HD), 0)
        rows.append(jnp.where(position < length, scaled, jnp.float32(0.0)))
    weights = jnp.concatenate(rows, 0)
    w_ref[...] = weights
    d_ref[...] = jnp.transpose(weights)[: od_ref.shape[0]] * od_ref[...]
    o_ref[...] = no_ref[...] * math.log2(math.e) + math.log2(slab)


def prep(per_rollout, slab, ids, lengths, advantages, adv_index, out_dot, norm_offset):
    heads, tokens = out_dot.shape
    scalars = pl.BlockSpec(memory_space=pltpu.SMEM)
    return pl.pallas_call(
        functools.partial(prep_kernel, per_rollout, slab),
        in_specs=[scalars] * 4 + [WHOLE] * 2,
        out_specs=[WHOLE] * 3,
        out_shape=[
            jax.ShapeDtypeStruct((tokens, HD), F32),
            jax.ShapeDtypeStruct((heads, tokens), F32),
            jax.ShapeDtypeStruct((heads, tokens), F32),
        ],
        compiler_params=pltpu.CompilerParams(vmem_limit_bytes=4 * MIB),
        cost_estimate=pl.CostEstimate(flops=2**30, bytes_accessed=0, transcendentals=0),
        name="prep",
    )(ids, lengths, advantages, adv_index, out_dot, norm_offset)


def heads_kernel(per_kv, off, q_ref, ct_ref, w_ref, o_ref, d_ref, kv_ref, dq_ref, grads_ref):
    tokens = q_ref.shape[0]
    pieces, _, rows, cols = kv_ref.shape
    count = cols // HD
    span = per_kv * HD
    scale = 1.0 / math.sqrt(HD)
    weights = w_ref[...]
    for g in range(count):
        head = (lax.axis_index("roll") ^ off) * count + g
        here = slice(g * HD, (g + 1) * HD)
        keys = jnp.concatenate([kv_ref[c, 0, :, here] for c in range(pieces)], 0)
        values = jnp.concatenate([kv_ref[c, 1, :, here] for c in range(pieces)], 0)
        places = [pl.ds(pl.multiple_of((head * per_kv + h) * HD, HD), HD) for h in range(per_kv)]
        q = jnp.concatenate([q_ref[:, c] for c in places], 0)
        go = jnp.concatenate([(ct_ref[:, c].astype(F32) * weights).astype(BF16) for c in places], 0)
        lines = pl.ds(pl.multiple_of(head * per_kv, per_kv), per_kv)
        offset = jnp.concatenate([o_ref[lines, :][h : h + 1] for h in range(per_kv)], 1)
        delta = jnp.concatenate([d_ref[lines, :][h : h + 1] for h in range(per_kv)], 1)
        scores = lax.dot_general(keys, q, NT, preferred_element_type=F32)
        prob = jnp.exp2(scores * (scale * math.log2(math.e)) - offset)
        dprob = lax.dot_general(values, go, NT, preferred_element_type=F32)
        dscore = ((prob * scale) * (dprob - delta)).astype(BF16)
        turned = jnp.dot(jnp.transpose(keys), dscore, preferred_element_type=F32).astype(BF16)
        for h in range(per_kv):
            dq_ref[:, g * span + h * HD : g * span + (h + 1) * HD] = jnp.transpose(
                turned[:, h * tokens : (h + 1) * tokens]
            )
        dk = jnp.dot(dscore, q, preferred_element_type=F32)
        dv = jnp.dot(prob.astype(BF16), go, preferred_element_type=F32)
        for c in range(pieces):
            part = slice(c * rows, (c + 1) * rows)
            grads_ref[c, 0, :, here] = dk[part].astype(grads_ref.dtype)
            grads_ref[c, 1, :, here] = dv[part].astype(grads_ref.dtype)


def head_block(off, kv_width, queries, cotangent, weights, offset, delta, kv, out_type):
    tokens, width = queries.shape
    pieces, _, rows, cols = kv.shape
    per_kv = width // kv_width
    slab = rows * pieces
    return pl.pallas_call(
        functools.partial(heads_kernel, per_kv, off),
        in_specs=[WHOLE] * 6,
        out_specs=[WHOLE, WHOLE],
        out_shape=[
            jax.ShapeDtypeStruct((tokens, per_kv * cols), BF16),
            jax.ShapeDtypeStruct((pieces, 2, rows, cols), out_type),
        ],
        compiler_params=pltpu.CompilerParams(vmem_limit_bytes=16 * MIB + slab * 32 * 1024),
        cost_estimate=pl.CostEstimate(
            flops=80 * tokens * per_kv * slab * cols, bytes_accessed=0, transcendentals=0
        ),
        name="head_block",
    )(queries, cotangent, weights, offset, delta, kv)


def finish(order, parts, own, received):
    tokens, span = parts[0].shape
    count = len(parts)

    def kernel(*refs):
        own_ref = refs[count]
        received_refs = refs[count + 1 : -4]
        out_ref, owned_ref, total_ref, sems = refs[-4:]
        roll = lax.axis_index("roll")
        copies = [
            pltpu.make_async_copy(
                refs[i],
                out_ref.at[:, pl.ds(pl.multiple_of((roll ^ order[i]) * span, span), span)],
                sems.at[i],
            )
            for i in range(count)
        ]
        for copy in copies:
            copy.start()
        total = own_ref[...]
        for ref in received_refs:
            total = total + ref[...].astype(F32)
        total_ref[...] = total
        copies.append(pltpu.make_async_copy(total_ref, owned_ref, sems.at[count]))
        copies[-1].start()
        for copy in copies:
            copy.wait()

    anywhere = pl.BlockSpec(memory_space=pl.ANY)
    return pl.pallas_call(
        kernel,
        in_specs=[anywhere] * count + [WHOLE] * (1 + len(received)),
        out_specs=[anywhere, anywhere],
        out_shape=[
            jax.ShapeDtypeStruct((tokens, span * count), BF16),
            jax.ShapeDtypeStruct(own.shape, F32),
        ],
        scratch_shapes=[pltpu.VMEM(own.shape, F32), pltpu.SemaphoreType.DMA((count + 1,))],
        compiler_params=pltpu.CompilerParams(vmem_limit_bytes=4 * MIB),
        cost_estimate=pl.CostEstimate(flops=2**30, bytes_accessed=0, transcendentals=0),
        name="finish",
    )(*parts, own, *received)


def add(wide, narrow, out_types, apart):
    count = len(narrow)

    def kernel(wide_ref, *refs):
        for k in range(wide.shape[0]) if apart else [slice(None)]:
            total = wide_ref[k]
            for ref in refs[:count]:
                total = total + ref[k].astype(F32)
            if apart:
                refs[count + k][...] = total.astype(out_types[k])
            else:
                for ref in refs[count:]:
                    ref[...] = total.astype(ref.dtype)

    shape = wide.shape[1:] if apart else wide.shape
    return pl.pallas_call(
        kernel,
        in_specs=[WHOLE] * (1 + count),
        out_specs=[WHOLE] * len(out_types),
        out_shape=[jax.ShapeDtypeStruct(shape, t) for t in out_types],
        compiler_params=pltpu.CompilerParams(vmem_limit_bytes=16 * MIB),
        cost_estimate=pl.CostEstimate(flops=2**28, bytes_accessed=0, transcendentals=0),
        name="add_sums",
    )(wide, *narrow)


def cut(x, count, shares):
    rows, width = x.shape
    span = width // (count * shares)

    def kernel(x_ref, *refs):
        part_refs, sems = refs[:-1], refs[-1]
        ctx = lax.axis_index("ctx")
        share = lax.axis_index("roll") % shares
        copies = [
            pltpu.make_async_copy(
                x_ref.at[:, pl.ds(pl.multiple_of((shares * (ctx ^ k) + share) * span, span), span)],
                part_refs[k],
                sems.at[k],
            )
            for k in range(count)
        ]
        for copy in copies:
            copy.start()
        for copy in copies:
            copy.wait()

    anywhere = pl.BlockSpec(memory_space=pl.ANY)
    return pl.pallas_call(
        kernel,
        in_specs=[anywhere],
        out_specs=[anywhere] * count,
        out_shape=[jax.ShapeDtypeStruct((rows, span), x.dtype)] * count,
        scratch_shapes=[pltpu.SemaphoreType.DMA((count,))],
        compiler_params=pltpu.CompilerParams(vmem_limit_bytes=4 * MIB),
        cost_estimate=pl.CostEstimate(flops=2**30, bytes_accessed=0, transcendentals=0),
        name="cut_hidden",
    )(x)


def turn(x):
    count = len(x)
    rows, cols = x[0].shape

    def kernel(*refs):
        refs[count][...] = jnp.transpose(jnp.concatenate([r[...] for r in refs[:count]], 0))

    return pl.pallas_call(
        kernel,
        in_specs=[WHOLE] * count,
        out_specs=WHOLE,
        out_shape=jax.ShapeDtypeStruct((cols, rows * count), BF16),
        compiler_params=pltpu.CompilerParams(vmem_limit_bytes=12 * MIB),
        cost_estimate=pl.CostEstimate(flops=2**29, bytes_accessed=0, transcendentals=0),
        name="turn_hidden",
    )(*x)


def weight_grads(offsets, shares, low):
    total = len(offsets)
    _, span, slab = shares[0].shape
    _, rows, cols = low[0].shape
    step = min(span, 512)
    steps = span // step
    slots = [(ref, i) for ref, x in enumerate(shares) for i in range(x.shape[0])]

    def kernel(*refs):
        x_refs = refs[: len(shares)]
        low_refs = refs[len(shares) : len(shares) + len(low)]
        out_ref, tiles, sems = refs[len(shares) + len(low) :]
        keys = jnp.concatenate([r[0] for r in low_refs], 0)
        values = jnp.concatenate([r[1] for r in low_refs], 0)
        mine = lax.axis_index("roll") % total
        copies = []
        for offset, (ref, i) in zip(offsets, slots, strict=True):
            for j in range(steps):
                n = len(copies)
                x = x_refs[ref][i, j * step : (j + 1) * step]
                tiles[n, 0] = jnp.dot(x, keys, preferred_element_type=F32)
                tiles[n, 1] = jnp.dot(x, values, preferred_element_type=F32)
                row = pl.multiple_of((mine ^ offset) * span + j * step, step)
                copies.append(
                    pltpu.make_async_copy(tiles.at[n], out_ref.at[:, pl.ds(row, step), :], sems.at[n])
                )
                copies[-1].start()
        for copy in copies:
            copy.wait()

    return pl.pallas_call(
        kernel,
        in_specs=[WHOLE] * (len(shares) + len(low)),
        out_specs=pl.BlockSpec(memory_space=pl.ANY),
        out_shape=jax.ShapeDtypeStruct((2, total * span, cols), F32),
        scratch_shapes=[
            pltpu.VMEM((total * steps, 2, step, cols), F32),
            pltpu.SemaphoreType.DMA((total * steps,)),
        ],
        compiler_params=pltpu.CompilerParams(vmem_limit_bytes=24 * MIB),
        cost_estimate=pl.CostEstimate(flops=2**31, bytes_accessed=0, transcendentals=0),
        name="weight_grads",
    )(*shares, *low)


def on_device(
    queries,
    cotangent,
    out_dot,
    norm_offset,
    prompt_kv,
    prompt_x,
    block_ids,
    lengths,
    advantages,
    adv_index,
):
    ctx_count = lax.axis_size("ctx")
    roll_count = lax.axis_size("roll")
    roll = lax.axis_index("roll")
    _, rows, kv_width = prompt_kv.shape
    cols = kv_width // roll_count
    slab = rows * ctx_count

    def to_ctx(x, offset):
        return lax.ppermute(x, "ctx", xor_pairs(ctx_count, offset))

    def to_roll(x, offset):
        return lax.ppermute(x, "roll", xor_pairs(roll_count, offset))

    last = roll_count - 1
    own = lax.dynamic_slice_in_dim(prompt_kv, (roll ^ last) * cols, cols, 2)
    fetched = jnp.stack([own] + [to_ctx(own, k) for k in range(1, ctx_count)])
    blocks = {last: fetched, last - 1: to_roll(fetched, 1)}
    for d in range(1, roll_count // 2):
        blocks[last - 2 * d] = to_roll(fetched, 2 * d)
        blocks[last - 2 * d - 1] = to_roll(blocks[last - 2 * d], 1)

    shares = roll_count
    while prompt_x.shape[1] // (ctx_count * shares) % HD:
        shares //= 2
    x_cut = cut(prompt_x, ctx_count, shares)
    out_dot, x_cut = lax.optimization_barrier((out_dot, x_cut))
    x_pieces = [x_cut[0]] + [to_ctx(x_cut[k], k) for k in range(1, ctx_count)]

    blocks_total = block_ids.shape[0] * ctx_count * roll_count
    weights, delta, offset = prep(
        blocks_total // lengths.shape[0], slab, block_ids, lengths, advantages, adv_index, out_dot.T, norm_offset.T
    )

    order = list(reversed(range(roll_count)))
    dq = []
    arrived = []
    for off in order:
        kind = BF16 if off % 2 else F32
        part, grads = head_block(
            off, kv_width, queries, cotangent, weights, offset, delta, blocks[off], kind
        )
        dq.append(part)
        if off == 1:
            x_pieces = lax.optimization_barrier((x_pieces, grads))[0]
            x_share = turn(x_pieces)[None]
        if off % 2:
            sibling = to_roll(grads, 1)
        elif off:
            (total,) = add(grads, [sibling], [BF16], False)
            delta, total = lax.optimization_barrier((delta, total))
            arrived.append(to_roll(total, off))
    sums = list(add(grads, [sibling] + arrived, [F32] + [BF16] * (ctx_count - 1), True))
    received = [to_ctx(sums[k], k) for k in range(1, ctx_count)]

    (owned_low,) = add(sums[0], received, [BF16], False)
    x_share = lax.optimization_barrier((x_share, sums[0]))[0]
    offsets, x_parts = [0], [x_share]
    bit = shares // 2
    while bit:
        whole = x_parts[0] if len(x_parts) == 1 else jnp.concatenate(x_parts)
        x_parts.append(to_roll(whole, bit))
        offsets += [offset ^ bit for offset in offsets]
        bit //= 2
        if bit:
            x_parts[-1] = lax.optimization_barrier((x_parts[-1], owned_low))[0]
    low = [owned_low] + [to_ctx(owned_low, k) for k in range(1, ctx_count)]
    dq, sums[0], owned_low = lax.optimization_barrier((dq, sums[0], owned_low))
    query_grad, owned = finish(order, dq, sums[0], received)
    return (query_grad, owned, weight_grads(offsets, x_parts, low))


def solution(mesh):
    placed = (
        P(("groups", "ctx", "roll"), None),
        P(("groups", "ctx", "roll"), None),
        P(("groups", "ctx", "roll"), None),
        P(("groups", "ctx", "roll"), None),
        P(None, ("groups", "ctx"), None),
        P(("groups", "ctx"), None),
        P(("groups", "ctx", "roll")),
        P("groups"),
        P("groups"),
        P("groups"),
    )
    return jax.shard_map(
        on_device,
        mesh=mesh,
        in_specs=placed,
        out_specs=(
            P(("groups", "ctx", "roll"), None),
            P(None, ("groups", "ctx"), "roll"),
            P(None, ("groups", "ctx"), "roll"),
        ),
        check_vma=False,
    )
```

```python
import functools
import math

import jax
import jax.numpy as jnp
from jax import lax
from jax.experimental import pallas as pl
from jax.experimental.pallas import tpu as pltpu
from jax.sharding import PartitionSpec as P

HD = 128
BLOCK = 32
MIB = 2**20
NT = (((1,), (1,)), ((), ()))
TN = (((0,), (0,)), ((), ()))
F32 = jnp.float32
BF16 = jnp.bfloat16
WHOLE = pl.BlockSpec(memory_space=pltpu.VMEM)


def xor_pairs(count, offset):
    return [(i, i ^ offset) for i in range(count)]


def prep_kernel(per_rollout, slab, ids, lengths, advantages, adv_index, od_ref, no_ref, w_ref, d_ref, o_ref):
    resp_max = per_rollout * BLOCK
    rows = []
    for b in range(ids.shape[0]):
        rollout = ids[b] // per_rollout
        slot = ids[b] % per_rollout
        length = lengths[rollout]
        scaled = jnp.full((BLOCK, HD), advantages[adv_index[rollout]] * resp_max, F32) / jnp.full(
            (BLOCK, HD), length.astype(F32), F32
        )
        position = slot * BLOCK + lax.broadcasted_iota(jnp.int32, (BLOCK, HD), 0)
        rows.append(jnp.where(position < length, scaled, jnp.float32(0.0)))
    weights = jnp.concatenate(rows, 0)
    w_ref[...] = weights
    d_ref[...] = jnp.transpose(weights)[: od_ref.shape[0]] * od_ref[...]
    o_ref[...] = no_ref[...] * math.log2(math.e) + math.log2(slab)


def prep(per_rollout, slab, ids, lengths, advantages, adv_index, out_dot, norm_offset):
    heads, tokens = out_dot.shape
    scalars = pl.BlockSpec(memory_space=pltpu.SMEM)
    return pl.pallas_call(
        functools.partial(prep_kernel, per_rollout, slab),
        in_specs=[scalars] * 4 + [WHOLE] * 2,
        out_specs=[WHOLE] * 3,
        out_shape=[
            jax.ShapeDtypeStruct((tokens, HD), F32),
            jax.ShapeDtypeStruct((heads, tokens), F32),
            jax.ShapeDtypeStruct((heads, tokens), F32),
        ],
        compiler_params=pltpu.CompilerParams(vmem_limit_bytes=4 * MIB),
        cost_estimate=pl.CostEstimate(flops=2**30, bytes_accessed=0, transcendentals=0),
        name="prep",
    )(ids, lengths, advantages, adv_index, out_dot, norm_offset)


def heads_kernel(per_kv, off, q_ref, ct_ref, w_ref, o_ref, d_ref, kv_ref, dq_ref, grads_ref):
    tokens = q_ref.shape[0]
    pieces, _, rows, cols = kv_ref.shape
    count = cols // HD
    span = per_kv * HD
    scale = 1.0 / math.sqrt(HD)
    weights = w_ref[...]
    for g in range(count):
        head = (lax.axis_index("roll") ^ off) * count + g
        here = slice(g * HD, (g + 1) * HD)
        keys = jnp.concatenate([kv_ref[c, 0, :, here] for c in range(pieces)], 0)
        values = jnp.concatenate([kv_ref[c, 1, :, here] for c in range(pieces)], 0)
        places = [pl.ds(pl.multiple_of((head * per_kv + h) * HD, HD), HD) for h in range(per_kv)]
        q = jnp.concatenate([q_ref[:, c] for c in places], 0)
        go = jnp.concatenate([(ct_ref[:, c].astype(F32) * weights).astype(BF16) for c in places], 0)
        lines = pl.ds(pl.multiple_of(head * per_kv, per_kv), per_kv)
        offset = jnp.concatenate([o_ref[lines, :][h : h + 1] for h in range(per_kv)], 1)
        delta = jnp.concatenate([d_ref[lines, :][h : h + 1] for h in range(per_kv)], 1)
        scores = lax.dot_general(keys, q, NT, preferred_element_type=F32)
        prob = jnp.exp2(scores * (scale * math.log2(math.e)) - offset)
        dprob = lax.dot_general(values, go, NT, preferred_element_type=F32)
        dscore = ((prob * scale) * (dprob - delta)).astype(BF16)
        dq = lax.dot_general(dscore, keys, TN, preferred_element_type=F32).astype(BF16)
        for h in range(per_kv):
            dq_ref[:, g * span + h * HD : g * span + (h + 1) * HD] = dq[h * tokens : (h + 1) * tokens]
        dk = jnp.dot(dscore, q, preferred_element_type=F32)
        dv = jnp.dot(prob.astype(BF16), go, preferred_element_type=F32)
        for c in range(pieces):
            part = slice(c * rows, (c + 1) * rows)
            grads_ref[c, 0, :, here] = dk[part].astype(grads_ref.dtype)
            grads_ref[c, 1, :, here] = dv[part].astype(grads_ref.dtype)


def head_block(off, kv_width, queries, cotangent, weights, offset, delta, kv, out_type):
    tokens, width = queries.shape
    pieces, _, rows, cols = kv.shape
    per_kv = width // kv_width
    slab = rows * pieces
    return pl.pallas_call(
        functools.partial(heads_kernel, per_kv, off),
        in_specs=[WHOLE] * 6,
        out_specs=[WHOLE, WHOLE],
        out_shape=[
            jax.ShapeDtypeStruct((tokens, per_kv * cols), BF16),
            jax.ShapeDtypeStruct((pieces, 2, rows, cols), out_type),
        ],
        compiler_params=pltpu.CompilerParams(vmem_limit_bytes=16 * MIB + slab * 32 * 1024),
        cost_estimate=pl.CostEstimate(
            flops=80 * tokens * per_kv * slab * cols, bytes_accessed=0, transcendentals=0
        ),
        name="head_block",
    )(queries, cotangent, weights, offset, delta, kv)


def finish(order, parts, own, received):
    tokens, span = parts[0].shape
    count = len(parts)

    def kernel(*refs):
        own_ref = refs[count]
        received_refs = refs[count + 1 : -4]
        out_ref, owned_ref, total_ref, sems = refs[-4:]
        roll = lax.axis_index("roll")
        copies = [
            pltpu.make_async_copy(
                refs[i],
                out_ref.at[:, pl.ds(pl.multiple_of((roll ^ order[i]) * span, span), span)],
                sems.at[i],
            )
            for i in range(count)
        ]
        for copy in copies:
            copy.start()
        total = own_ref[...]
        for ref in received_refs:
            total = total + ref[...].astype(F32)
        total_ref[...] = total
        copies.append(pltpu.make_async_copy(total_ref, owned_ref, sems.at[count]))
        copies[-1].start()
        for copy in copies:
            copy.wait()

    anywhere = pl.BlockSpec(memory_space=pl.ANY)
    return pl.pallas_call(
        kernel,
        in_specs=[anywhere] * count + [WHOLE] * (1 + len(received)),
        out_specs=[anywhere, anywhere],
        out_shape=[
            jax.ShapeDtypeStruct((tokens, span * count), BF16),
            jax.ShapeDtypeStruct(own.shape, F32),
        ],
        scratch_shapes=[pltpu.VMEM(own.shape, F32), pltpu.SemaphoreType.DMA((count + 1,))],
        compiler_params=pltpu.CompilerParams(vmem_limit_bytes=4 * MIB),
        cost_estimate=pl.CostEstimate(flops=2**30, bytes_accessed=0, transcendentals=0),
        name="finish",
    )(*parts, own, *received)


def add(wide, narrow, out_types, apart):
    count = len(narrow)

    def kernel(wide_ref, *refs):
        for k in range(wide.shape[0]) if apart else [slice(None)]:
            total = wide_ref[k]
            for ref in refs[:count]:
                total = total + ref[k].astype(F32)
            if apart:
                refs[count + k][...] = total.astype(out_types[k])
            else:
                for ref in refs[count:]:
                    ref[...] = total.astype(ref.dtype)

    shape = wide.shape[1:] if apart else wide.shape
    return pl.pallas_call(
        kernel,
        in_specs=[WHOLE] * (1 + count),
        out_specs=[WHOLE] * len(out_types),
        out_shape=[jax.ShapeDtypeStruct(shape, t) for t in out_types],
        compiler_params=pltpu.CompilerParams(vmem_limit_bytes=16 * MIB),
        cost_estimate=pl.CostEstimate(flops=2**28, bytes_accessed=0, transcendentals=0),
        name="add_sums",
    )(wide, *narrow)


def cut(x, count, shares):
    rows, width = x.shape
    span = width // (count * shares)

    def kernel(x_ref, *refs):
        part_refs, sems = refs[:-1], refs[-1]
        ctx = lax.axis_index("ctx")
        share = lax.axis_index("roll") % shares
        copies = [
            pltpu.make_async_copy(
                x_ref.at[:, pl.ds(pl.multiple_of((shares * (ctx ^ k) + share) * span, span), span)],
                part_refs[k],
                sems.at[k],
            )
            for k in range(count)
        ]
        for copy in copies:
            copy.start()
        for copy in copies:
            copy.wait()

    anywhere = pl.BlockSpec(memory_space=pl.ANY)
    return pl.pallas_call(
        kernel,
        in_specs=[anywhere],
        out_specs=[anywhere] * count,
        out_shape=[jax.ShapeDtypeStruct((rows, span), x.dtype)] * count,
        scratch_shapes=[pltpu.SemaphoreType.DMA((count,))],
        compiler_params=pltpu.CompilerParams(vmem_limit_bytes=4 * MIB),
        cost_estimate=pl.CostEstimate(flops=2**30, bytes_accessed=0, transcendentals=0),
        name="cut_hidden",
    )(x)


def turn(x):
    count = len(x)
    rows, cols = x[0].shape

    def kernel(*refs):
        refs[count][...] = jnp.transpose(jnp.concatenate([r[...] for r in refs[:count]], 0))

    return pl.pallas_call(
        kernel,
        in_specs=[WHOLE] * count,
        out_specs=WHOLE,
        out_shape=jax.ShapeDtypeStruct((cols, rows * count), BF16),
        compiler_params=pltpu.CompilerParams(vmem_limit_bytes=12 * MIB),
        cost_estimate=pl.CostEstimate(flops=2**29, bytes_accessed=0, transcendentals=0),
        name="turn_hidden",
    )(*x)


def weight_grads(offsets, shares, low):
    total = len(offsets)
    _, span, slab = shares[0].shape
    _, rows, cols = low[0].shape
    step = min(span, 512)
    steps = span // step
    slots = [(ref, i) for ref, x in enumerate(shares) for i in range(x.shape[0])]

    def kernel(*refs):
        x_refs = refs[: len(shares)]
        low_refs = refs[len(shares) : len(shares) + len(low)]
        out_ref, tiles, sems = refs[len(shares) + len(low) :]
        keys = jnp.concatenate([r[0] for r in low_refs], 0)
        values = jnp.concatenate([r[1] for r in low_refs], 0)
        mine = lax.axis_index("roll") % total
        copies = []
        for offset, (ref, i) in zip(offsets, slots, strict=True):
            for j in range(steps):
                n = len(copies)
                x = x_refs[ref][i, j * step : (j + 1) * step]
                tiles[n, 0] = jnp.dot(x, keys, preferred_element_type=F32)
                tiles[n, 1] = jnp.dot(x, values, preferred_element_type=F32)
                row = pl.multiple_of((mine ^ offset) * span + j * step, step)
                copies.append(
                    pltpu.make_async_copy(tiles.at[n], out_ref.at[:, pl.ds(row, step), :], sems.at[n])
                )
                copies[-1].start()
        for copy in copies:
            copy.wait()

    return pl.pallas_call(
        kernel,
        in_specs=[WHOLE] * (len(shares) + len(low)),
        out_specs=pl.BlockSpec(memory_space=pl.ANY),
        out_shape=jax.ShapeDtypeStruct((2, total * span, cols), F32),
        scratch_shapes=[
            pltpu.VMEM((total * steps, 2, step, cols), F32),
            pltpu.SemaphoreType.DMA((total * steps,)),
        ],
        compiler_params=pltpu.CompilerParams(vmem_limit_bytes=24 * MIB),
        cost_estimate=pl.CostEstimate(flops=2**31, bytes_accessed=0, transcendentals=0),
        name="weight_grads",
    )(*shares, *low)


def on_device(
    queries,
    cotangent,
    out_dot,
    norm_offset,
    prompt_kv,
    prompt_x,
    block_ids,
    lengths,
    advantages,
    adv_index,
):
    ctx_count = lax.axis_size("ctx")
    roll_count = lax.axis_size("roll")
    roll = lax.axis_index("roll")
    _, rows, kv_width = prompt_kv.shape
    cols = kv_width // roll_count
    slab = rows * ctx_count

    def to_ctx(x, offset):
        return lax.ppermute(x, "ctx", xor_pairs(ctx_count, offset))

    def to_roll(x, offset):
        return lax.ppermute(x, "roll", xor_pairs(roll_count, offset))

    last = roll_count - 1
    own = lax.dynamic_slice_in_dim(prompt_kv, (roll ^ last) * cols, cols, 2)
    fetched = jnp.stack([own] + [to_ctx(own, k) for k in range(1, ctx_count)])
    blocks = {last: fetched, last - 1: to_roll(fetched, 1)}
    for d in range(1, roll_count // 2):
        blocks[last - 2 * d] = to_roll(fetched, 2 * d)
        blocks[last - 2 * d - 1] = to_roll(blocks[last - 2 * d], 1)

    shares = roll_count
    while prompt_x.shape[1] // (ctx_count * shares) % HD:
        shares //= 2
    x_cut = cut(prompt_x, ctx_count, shares)
    out_dot, x_cut = lax.optimization_barrier((out_dot, x_cut))
    x_pieces = [x_cut[0]] + [to_ctx(x_cut[k], k) for k in range(1, ctx_count)]

    blocks_total = block_ids.shape[0] * ctx_count * roll_count
    weights, delta, offset = prep(
        blocks_total // lengths.shape[0], slab, block_ids, lengths, advantages, adv_index, out_dot.T, norm_offset.T
    )

    order = list(reversed(range(roll_count)))
    dq = []
    arrived = []
    for off in order:
        kind = BF16 if off % 2 else F32
        part, grads = head_block(
            off, kv_width, queries, cotangent, weights, offset, delta, blocks[off], kind
        )
        dq.append(part)
        if off == 1:
            x_pieces = lax.optimization_barrier((x_pieces, grads))[0]
            x_share = turn(x_pieces)[None]
        if off % 2:
            sibling = to_roll(grads, 1)
        elif off:
            (total,) = add(grads, [sibling], [BF16], False)
            delta, total = lax.optimization_barrier((delta, total))
            arrived.append(to_roll(total, off))
    sums = list(add(grads, [sibling] + arrived, [F32] + [BF16] * (ctx_count - 1), True))
    received = [to_ctx(sums[k], k) for k in reversed(range(1, ctx_count))]

    (owned_low,) = add(sums[0], received, [BF16], False)
    x_share = lax.optimization_barrier((x_share, sums[0]))[0]
    offsets, x_parts = [0], [x_share]
    bit = shares // 2
    while bit:
        whole = x_parts[0] if len(x_parts) == 1 else jnp.concatenate(x_parts)
        x_parts.append(to_roll(whole, bit))
        offsets += [offset ^ bit for offset in offsets]
        bit //= 2
        if bit:
            x_parts[-1] = lax.optimization_barrier((x_parts[-1], owned_low))[0]
    low = [owned_low] + [to_ctx(owned_low, k) for k in reversed(range(1, ctx_count))][::-1]
    dq, sums[0], owned_low = lax.optimization_barrier((dq, sums[0], owned_low))
    query_grad, owned = finish(order, dq, sums[0], received)
    return (query_grad, owned, weight_grads(offsets, x_parts, low))


def solution(mesh):
    placed = (
        P(("groups", "ctx", "roll"), None),
        P(("groups", "ctx", "roll"), None),
        P(("groups", "ctx", "roll"), None),
        P(("groups", "ctx", "roll"), None),
        P(None, ("groups", "ctx"), None),
        P(("groups", "ctx"), None),
        P(("groups", "ctx", "roll")),
        P("groups"),
        P("groups"),
        P("groups"),
    )
    return jax.shard_map(
        on_device,
        mesh=mesh,
        in_specs=placed,
        out_specs=(
            P(("groups", "ctx", "roll"), None),
            P(None, ("groups", "ctx"), "roll"),
            P(None, ("groups", "ctx"), "roll"),
        ),
        check_vma=False,
    )
```
